256 devices in a mesh: lon: 16 (over y_hi, z), lat: 16 (over y_lo, x, core).
Axes of the slice: x: 4, y: 4 (y_hi: 2, y_lo: 2; y = y_hi * 2 + y_lo), z: 8, core: 2. Of those that a mesh axis runs over, the one named last changes fastest.
Arguments:
- ocean_state: bfloat16 [200, 128, 2048], P(None, 'lat', 'lon'), may hold values from -6 to 6
- land_sea: int32 [128, 2048], P('lat', 'lon'), may hold values 0 or 1
- depth_kernel: bfloat16 [49, 200], replicated, may hold values from -0.875 to 0.875
- norm_gain: float32 [200], replicated, may hold values from 0.1 to 1.9
- w_expand: bfloat16 [800, 200], replicated, may hold values from -0.4375 to 0.4375
- b_expand: float32 [800], replicated, may hold values from -3 to 3
- w_project: bfloat16 [800, 200], replicated, may hold values from -0.21875 to 0.21875
- cotangent: bfloat16 [200, 128, 2048], P(None, 'lat', 'lon'), may hold values from -6 to 6
Outputs:
- next_state: bfloat16 [200, 128, 2048], P(None, 'lat', 'lon')
- grad_state: bfloat16 [200, 128, 2048], P(None, 'lat', 'lon')
- grad_kernel: float32 [49, 200], replicated
- grad_gain: float32 [200], replicated
- grad_expand: float32 [800, 200], P('lon')
- grad_project: float32 [800, 200], P('lon')
- grad_bias: float32 [800], P('lon')
The draws below stay inside these ranges and needn't reach their ends.
All inputs are finite; a program needn't handle non-finite values. No bound on the sum of `land_sea` on one device may be relied on, other than what follows from the above.
Results may differ from the reference program's by a relative error of at most 0.014.
Values may be sent and summed in bfloat16 or wider, within the bound.
No kernel may reach another device: no remote copies, remote signals or barrier semaphores. Data moves between devices by JAX's collectives and lax.ppermute only.
A program may use at most 64 MiB of HBM per device.

```python
import jax
import jax.numpy as jnp
from jax import lax

C = 200
HID = 800
TAPS = 49
ROWS_DEV = 8
ROWS = 128
LON = 2048
N_LAT = 16


def set_ends(result, rng, smallest, top_value):
    extent = result.shape
    index_at = [jax.random.randint(jax.random.fold_in(rng, axis), (), 0, extent[axis]) for axis in range(len(extent))]
    result = result.at[tuple(index_at)].set(smallest)
    longest = extent.index(max(extent))
    index_at[longest] = (index_at[longest] + 1) % extent[longest]
    return result.at[tuple(index_at)].set(top_value)


def levels(stream_key, shape, shards, smallest, largest):
    loudness, own = 1.0, jax.random.fold_in(stream_key, 6)
    for position, parts in shards:
        heights = jnp.exp(jax.random.uniform(jax.random.fold_in(own, position), (parts,), jnp.float32, smallest / len(shards), largest / len(shards)))
        loudness = loudness * jnp.repeat(heights, shape[position] // parts).reshape([-1 if axis == position else 1 for axis in range(len(shape))])
    return loudness


def scatter_about(stream_key, dims, scale, bound, pieces=(), kind=jnp.bfloat16):
    entries = scale * jax.random.normal(stream_key, dims, jnp.float32)
    if pieces:
        entries = entries * levels(stream_key, dims, pieces, -0.22, 0.18)
    return jnp.clip(entries, -bound, bound).astype(kind)


def setup_inputs(seed: int = 0) -> dict:
    streams_of = jax.random.split(jax.random.key(seed), 9)
    return {
        "ocean_state": scatter_about(streams_of[0], (C, ROWS, LON), 1.0, 6.0, ((1, 16), (2, 16))),
        "land_sea": set_ends((jax.random.randint(streams_of[1], (ROWS, LON), 0, 4) < 3).astype(jnp.int32), jax.random.fold_in(streams_of[1], 1), 0, 1),
        "depth_kernel": scatter_about(streams_of[2], (TAPS, C), TAPS ** -0.5, 0.875),
        "norm_gain": jnp.clip(1.0 + 0.18 * jax.random.normal(streams_of[3], (C,), jnp.float32), 0.1, 1.9),
        "w_expand": scatter_about(streams_of[4], (HID, C), C ** -0.5, 0.4375),
        "b_expand": scatter_about(streams_of[5], (HID,), 0.5, 3.0, (), jnp.float32),
        "w_project": scatter_about(streams_of[6], (HID, C), HID ** -0.5, 0.21875),
        "cotangent": scatter_about(streams_of[7], (C, ROWS, LON), 1.0, 6.0, ((1, 16), (2, 16))),
    }


EPS = 1e-06

def gelu_pair(inner):
    normal_cdf = 0.5 * (1.0 + lax.erf(inner * 0.7071067811865476))
    density = jnp.exp(-0.5 * inner * inner) * 0.3989422804014327
    return (inner * normal_cdf, normal_cdf + inner * density)

def wrap_pad(masked):
    wide = jnp.concatenate([masked[:, :, -3:], masked, masked[:, :, :3]], axis=2)
    return jnp.pad(wide, ((0, 0), (3, 3), (0, 0)))

def depthwise(padded, kernel, row_count, col_count, flipped):
    total = jnp.zeros((padded.shape[0], row_count, col_count), jnp.float32)
    for row_tap in range(7):
        for col_tap in range(7):
            weight = kernel[row_tap * 7 + col_tap].astype(jnp.float32)[:, None, None]
            row_start = 6 - row_tap if flipped else row_tap
            col_start = 6 - col_tap if flipped else col_tap
            window = padded[:, row_start:row_start + row_count, col_start:col_start + col_count]
            total = total + weight * window.astype(jnp.float32)
    return total

def kernel_grad(padded, upstream, row_count, col_count):
    rows_out = []
    for row_tap in range(7):
        for col_tap in range(7):
            window = padded[:, row_tap:row_tap + row_count, col_tap:col_tap + col_count]
            rows_out.append(lax.optimization_barrier(jnp.sum(upstream * window.astype(jnp.float32), axis=(1, 2))))
    return jnp.stack(rows_out, axis=0)

def cell_part(state_cells, mixed_cells, mask_cells, cot_cells, norm_gain, w_expand, b_expand, w_project):
    center = lax.optimization_barrier(jnp.mean(mixed_cells, axis=0, keepdims=True))
    centered = mixed_cells - center
    inv_spread = lax.rsqrt(lax.optimization_barrier(jnp.mean(centered * centered, axis=0, keepdims=True)) + EPS)
    whitened = centered * inv_spread
    normed = (whitened * norm_gain[:, None]).astype(jnp.bfloat16)
    hidden_in = jnp.dot(w_expand, normed, preferred_element_type=jnp.float32) + b_expand[:, None]
    gelu_value, gelu_slope = gelu_pair(hidden_in)
    activ = gelu_value.astype(jnp.bfloat16)
    branch = lax.dot_general(w_project, activ, (((0,), (0,)), ((), ())), preferred_element_type=jnp.float32)
    mask_float = mask_cells.astype(jnp.float32)[None]
    next_cells = (mask_float * (state_cells.astype(jnp.float32) + branch)).astype(jnp.bfloat16)
    gated = (cot_cells.astype(jnp.float32) * mask_float).astype(jnp.bfloat16)
    back_act = jnp.dot(w_project, gated, preferred_element_type=jnp.float32)
    back_in = (back_act * gelu_slope).astype(jnp.bfloat16)
    bias_term = lax.optimization_barrier(jnp.sum(back_in.astype(jnp.float32), axis=1))
    back_norm = lax.dot_general(w_expand, back_in, (((0,), (0,)), ((), ())), preferred_element_type=jnp.float32)
    gain_term = lax.optimization_barrier(jnp.sum(back_norm * whitened, axis=1))
    scaled = back_norm * norm_gain[:, None]
    back_mixed = inv_spread * (scaled - lax.optimization_barrier(jnp.mean(scaled, axis=0, keepdims=True)) - whitened * lax.optimization_barrier(jnp.mean(scaled * whitened, axis=0, keepdims=True)))
    return (next_cells, back_mixed.astype(jnp.bfloat16), activ, gated, back_in, normed, bias_term, gain_term)

def reference(ocean_state, land_sea, depth_kernel, norm_gain, w_expand, b_expand, w_project, cotangent):
    channels = ocean_state.shape[0]
    row_total = ocean_state.shape[1]
    col_total = ocean_state.shape[2]
    block_cells = ROWS_DEV * col_total
    mask_bf = land_sea.astype(jnp.bfloat16)
    masked = ocean_state * mask_bf[None]
    padded = wrap_pad(masked)
    mixed_field = depthwise(padded, depth_kernel, row_total, col_total, False)

    def to_blocks(array):
        return jnp.transpose(array.reshape(channels, N_LAT, block_cells), (1, 0, 2))

    def one_block(carry, items):
        state_cells, mixed_cells, mask_cells, cot_cells = items
        outs = cell_part(state_cells, mixed_cells, mask_cells, cot_cells, norm_gain, w_expand, b_expand, w_project)
        next_cells, back_cells, activ, gated, back_in, normed, bias_term, gain_term = outs
        proj_term = lax.dot_general(activ, gated, (((1,), (1,)), ((), ())), preferred_element_type=jnp.float32)
        expand_term = lax.dot_general(back_in, normed, (((1,), (1,)), ((), ())), preferred_element_type=jnp.float32)
        carry = (carry[0] + expand_term, carry[1] + proj_term, carry[2] + bias_term, carry[3] + gain_term)
        return (carry, (next_cells, back_cells))
    hidden_units = w_expand.shape[0]
    start_carry = (jnp.zeros((hidden_units, channels), jnp.float32), jnp.zeros((hidden_units, channels), jnp.float32), jnp.zeros((hidden_units,), jnp.float32), jnp.zeros((channels,), jnp.float32))
    items = (to_blocks(ocean_state), to_blocks(mixed_field), land_sea.reshape(N_LAT, block_cells), to_blocks(cotangent))
    totals, stacked = lax.scan(one_block, start_carry, items)
    grad_expand, grad_project, grad_bias, grad_gain = totals

    def from_blocks(array):
        return jnp.transpose(array, (1, 0, 2)).reshape(channels, row_total, col_total)
    next_state = from_blocks(stacked[0])
    back_mixed = from_blocks(stacked[1])
    grad_kernel = kernel_grad(padded, back_mixed.astype(jnp.float32), row_total, col_total)
    back_masked = depthwise(wrap_pad(back_mixed), depth_kernel, row_total, col_total, True)
    mask_float = land_sea.astype(jnp.float32)[None]
    grad_state = (mask_float * (cotangent.astype(jnp.float32) + back_masked)).astype(jnp.bfloat16)
    return (next_state, grad_state, grad_kernel, grad_gain, grad_expand, grad_project, grad_bias)
```

```python
import jax
import jax.numpy as jnp
from jax import lax
from jax.sharding import PartitionSpec as P

EPS = 1e-06


def with_halo(value, sides, width, wrap):
    for axis, dim in sides:
        size, length = (lax.axis_size(axis), value.shape[dim])
        up = [(i, (i + 1) % size) for i in range(size if wrap else size - 1)]
        down = [(j, i) for i, j in up]
        last = lax.slice_in_dim(value, length - width, length, axis=dim)
        initial = lax.slice_in_dim(value, 0, width, axis=dim)
        before = lax.ppermute(last, axis, up)
        after = lax.ppermute(initial, axis, down)
        value = jnp.concatenate([before, value, after], axis=dim)
    return value


def gelu_pair(inner):
    normal_cdf = 0.5 * (1.0 + lax.erf(inner * 0.7071067811865476))
    density = jnp.exp(-0.5 * inner * inner) * 0.3989422804014327
    return (inner * normal_cdf, normal_cdf + inner * density)


def extend(field):
    wide = with_halo(field, (("lon", 2),), 3, True)
    return with_halo(wide, (("lat", 1),), 3, False)


def depthwise(padded, kernel, row_count, col_count, flipped):
    total = jnp.zeros((padded.shape[0], row_count, col_count), jnp.float32)
    for row_tap in range(7):
        for col_tap in range(7):
            weight = kernel[row_tap * 7 + col_tap].astype(jnp.float32)[:, None, None]
            row_start = 6 - row_tap if flipped else row_tap
            col_start = 6 - col_tap if flipped else col_tap
            window = padded[:, row_start : row_start + row_count, col_start : col_start + col_count]
            total = total + weight * window.astype(jnp.float32)
    return total


def kernel_grad(padded, upstream, row_count, col_count):
    rows_out = []
    for row_tap in range(7):
        for col_tap in range(7):
            window = padded[:, row_tap : row_tap + row_count, col_tap : col_tap + col_count]
            rows_out.append(jnp.sum(upstream * window.astype(jnp.float32), axis=(1, 2)))
    return jnp.stack(rows_out, axis=0)


def cell_part(
    state_cells, mixed_cells, mask_cells, cot_cells, norm_gain, w_expand, b_expand, w_project
):
    center = jnp.mean(mixed_cells, axis=0, keepdims=True)
    centered = mixed_cells - center
    inv_spread = lax.rsqrt(jnp.mean(centered * centered, axis=0, keepdims=True) + EPS)
    whitened = centered * inv_spread
    normed = (whitened * norm_gain[:, None]).astype(jnp.bfloat16)
    hidden_in = jnp.dot(w_expand, normed, preferred_element_type=jnp.float32) + b_expand[:, None]
    gelu_value, gelu_slope = gelu_pair(hidden_in)
    activ = gelu_value.astype(jnp.bfloat16)
    branch = lax.dot_general(
        w_project, activ, (((0,), (0,)), ((), ())), preferred_element_type=jnp.float32
    )
    mask_float = mask_cells.astype(jnp.float32)[None]
    next_cells = (mask_float * (state_cells.astype(jnp.float32) + branch)).astype(jnp.bfloat16)
    gated = (cot_cells.astype(jnp.float32) * mask_float).astype(jnp.bfloat16)
    back_act = jnp.dot(w_project, gated, preferred_element_type=jnp.float32)
    back_in = (back_act * gelu_slope).astype(jnp.bfloat16)
    bias_term = jnp.sum(back_in.astype(jnp.float32), axis=1)
    back_norm = lax.dot_general(
        w_expand, back_in, (((0,), (0,)), ((), ())), preferred_element_type=jnp.float32
    )
    gain_term = jnp.sum(back_norm * whitened, axis=1)
    scaled = back_norm * norm_gain[:, None]
    back_mixed = inv_spread * (
        scaled
        - jnp.mean(scaled, axis=0, keepdims=True)
        - whitened * jnp.mean(scaled * whitened, axis=0, keepdims=True)
    )
    return (
        next_cells,
        back_mixed.astype(jnp.bfloat16),
        activ,
        gated,
        back_in,
        normed,
        bias_term,
        gain_term,
    )


def reduce_grads(expand, project, bias, gain, taps):
    hidden, channels = expand.shape
    n_lon, n_lat = lax.axis_size("lon"), lax.axis_size("lat")
    share = hidden // n_lon
    first_core = lax.axis_index("lat") % 2 == 0
    swap = [(i, i ^ 1) for i in range(n_lat)]
    tap_rows = jnp.concatenate([taps, gain[None]], axis=0)
    half_rows = tap_rows.shape[0] // 2
    pad = jnp.zeros((hidden, 1), jnp.float32)
    full_a = jnp.concatenate([expand, bias[:, None]], axis=1)
    full_b = jnp.concatenate([project, pad], axis=1)
    taps_a = jnp.pad(tap_rows[:half_rows], ((0, 0), (0, 1)))
    taps_b = jnp.pad(tap_rows[half_rows:], ((0, 0), (0, 1)))

    def halve(one, two):
        own = jnp.where(first_core, one, two)
        other = jnp.where(first_core, two, one).astype(jnp.bfloat16)
        return own + lax.ppermute(other, "lat", swap).astype(jnp.float32)

    weights = halve(full_a, full_b).astype(jnp.bfloat16).reshape(n_lon, share, channels + 1)
    taps_own = halve(taps_a, taps_b).astype(jnp.bfloat16)
    parts = jnp.concatenate(
        [weights, jnp.broadcast_to(taps_own, (n_lon, *taps_own.shape))], axis=1
    )
    parts = lax.all_to_all(parts, "lon", 0, 0)
    own = jnp.sum(parts.astype(jnp.float32), axis=0).astype(jnp.bfloat16)
    groups = [list(range(core, n_lat, 2)) for core in range(2)]
    spread = jnp.broadcast_to(own, (n_lat // 2, *own.shape))
    spread = lax.all_to_all(spread, "lat", 0, 0, axis_index_groups=groups)
    own = jnp.sum(spread.astype(jnp.float32), axis=0).astype(jnp.bfloat16)
    other = lax.ppermute(own, "lat", swap)
    part_a = jnp.where(first_core, own, other).astype(jnp.float32)
    part_b = jnp.where(first_core, other, own).astype(jnp.float32)
    tap_sums = jnp.concatenate([part_a[share:], part_b[share:]], axis=0)[:, :channels]
    return (
        part_a[:share, :channels],
        part_b[:share, :channels],
        part_a[:share, channels],
        tap_sums[-1],
        tap_sums[:-1],
    )


def shards(
    ocean_state, land_sea, depth_kernel, norm_gain, w_expand, b_expand, w_project, cotangent
):
    channels, row_count, col_count = ocean_state.shape
    cell_count = row_count * col_count
    hidden_units = w_expand.shape[0]
    masked = ocean_state * land_sea.astype(jnp.bfloat16)[None]
    padded = extend(masked)
    mixed_field = depthwise(padded, depth_kernel, row_count, col_count, False)
    outs = cell_part(
        ocean_state.reshape(channels, cell_count),
        mixed_field.reshape(channels, cell_count),
        land_sea.reshape(cell_count),
        cotangent.reshape(channels, cell_count),
        norm_gain,
        w_expand,
        b_expand,
        w_project,
    )
    next_cells, back_cells, activ, gated, back_in, normed, bias_term, gain_term = outs
    next_state = next_cells.reshape(channels, row_count, col_count)
    back_mixed = back_cells.reshape(channels, row_count, col_count)
    kernel_term = kernel_grad(padded, back_mixed.astype(jnp.float32), row_count, col_count)
    back_masked = depthwise(extend(back_mixed), depth_kernel, row_count, col_count, True)
    mask_float = land_sea.astype(jnp.float32)[None]
    grad_state = (mask_float * (cotangent.astype(jnp.float32) + back_masked)).astype(jnp.bfloat16)
    proj_term = lax.dot_general(
        activ, gated, (((1,), (1,)), ((), ())), preferred_element_type=jnp.float32
    )
    expand_term = lax.dot_general(
        back_in, normed, (((1,), (1,)), ((), ())), preferred_element_type=jnp.float32
    )
    grad_expand, grad_project, grad_bias, grad_gain, grad_kernel = reduce_grads(
        expand_term, proj_term, bias_term, gain_term, kernel_term
    )
    return (next_state, grad_state, grad_kernel, grad_gain, grad_expand, grad_project, grad_bias)


def solution(mesh):
    placed = (
        P(None, "lat", "lon"),
        P("lat", "lon"),
        P(),
        P(),
        P(),
        P(),
        P(),
        P(None, "lat", "lon"),
    )
    return jax.shard_map(
        shards,
        mesh=mesh,
        in_specs=placed,
        out_specs=(
            P(None, "lat", "lon"),
            P(None, "lat", "lon"),
            P(),
            P(),
            P("lon", None),
            P("lon", None),
            P("lon"),
        ),
        check_vma=False,
    )
```

```python
import functools

import jax
import jax.numpy as jnp
from jax import lax
from jax.experimental import pallas as pl
from jax.experimental.pallas import tpu as pltpu
from jax.sharding import PartitionSpec as P

EPS = 1e-06
BF = jnp.bfloat16
F32 = jnp.float32
HALO = 3
TAPS = 7
VMEM_BYTES = 24 * 1024 * 1024


def kernel_call(body, outs, scratch=(), n_in=0, n_any=0, micros=1):
    specs = [pl.BlockSpec(memory_space=pltpu.HBM)] * n_any
    specs += [pl.BlockSpec(memory_space=pltpu.VMEM)] * n_in
    return pl.pallas_call(
        body,
        out_shape=[jax.ShapeDtypeStruct(shape, dtype) for shape, dtype in outs],
        in_specs=specs,
        out_specs=[pl.BlockSpec(memory_space=pltpu.VMEM)] * len(outs),
        scratch_shapes=list(scratch),
        compiler_params=pltpu.CompilerParams(vmem_limit_bytes=VMEM_BYTES),
        cost_estimate=pl.CostEstimate(
            flops=micros * 1_000_000_000, bytes_accessed=micros * 3_000_000, transcendentals=0
        ),
    )


def nt_dot(left, right):
    return lax.dot_general(left, right, (((1,), (1,)), ((), ())), preferred_element_type=F32)


def tn_dot(left, right):
    return lax.dot_general(left, right, (((0,), (0,)), ((), ())), preferred_element_type=F32)


def dot(left, right):
    return jnp.dot(left, right, preferred_element_type=F32)


def load_masked(field_hbm, mask_hbm, field, mask_ref, flat, sems):
    channels, rows, lanes = field.shape
    parts = sems.shape[0] - 1
    step = channels // parts
    copies = [pltpu.make_async_copy(mask_hbm, mask_ref, sems.at[parts])]
    for k in range(parts):
        part = pl.ds(k * step, step)
        copies.append(pltpu.make_async_copy(field_hbm.at[part], field.at[part], sems.at[k]))
    for copy in copies:
        copy.start()
    for copy in copies:
        copy.wait()
    mask = mask_ref[...].astype(F32)[None]
    flat[...] = (field[...].astype(F32) * mask).reshape(channels * rows, lanes)
    return [flat[pl.ds(row, channels, stride=rows), :].astype(BF) for row in range(rows)]


def state_body(x_hbm, mask_hbm, m_ref, top_ref, bot_ref, field, mask_ref, flat, sems):
    masked = load_masked(x_hbm, mask_hbm, field, mask_ref, flat, sems)
    rows = len(masked)
    for row, value in enumerate(masked):
        m_ref[row] = value
        if row < HALO:
            top_ref[row] = value
        if row >= rows - HALO:
            bot_ref[row - rows + HALO] = value


def gated_body(cot_hbm, mask_hbm, g_ref, field, mask_ref, flat, sems):
    for row, value in enumerate(load_masked(cot_hbm, mask_hbm, field, mask_ref, flat, sems)):
        g_ref[row] = value


def columns(row, lanes):
    high = row.astype(BF)
    rest = row - high.astype(F32)
    middle = rest.astype(BF)
    low = (rest - middle.astype(F32)).astype(BF)
    spare = jnp.zeros((5, row.shape[1]), F32)
    parts = [high.astype(F32), middle.astype(F32), low.astype(F32), spare]
    parts = jnp.concatenate(parts, axis=0).astype(BF)
    return tn_dot(parts, jnp.ones((8, lanes), BF))


def weights_body(
    taps_ref, gain_ref, bias_ref, we_ref, wp_ref, spread_ref, gains_ref, biases_ref, we_t_ref, wp_t_ref
):
    count, channels, lanes = spread_ref.shape
    unit = lax.broadcasted_iota(jnp.int32, (count, lanes), 0)
    unit = unit == lax.broadcasted_iota(jnp.int32, (count, lanes), 1)
    taps = tn_dot(taps_ref[...], jnp.where(unit, 1.0, 0.0).astype(BF))
    for tap in range(count):
        spread_ref[tap] = jnp.broadcast_to(taps[:, tap : tap + 1], (channels, lanes))
    gains_ref[...] = columns(gain_ref[...], lanes)
    biases_ref[...] = columns(bias_ref[...], lanes)
    eye = lax.broadcasted_iota(jnp.int32, (channels, channels), 0)
    eye = eye == lax.broadcasted_iota(jnp.int32, (channels, channels), 1)
    eye = jnp.where(eye, 1.0, 0.0).astype(BF)
    we_t_ref[...] = nt_dot(eye, we_ref[...]).astype(BF)
    wp_t_ref[...] = nt_dot(eye, wp_ref[...]).astype(BF)


def is_first(place_ref, shape):
    return jnp.broadcast_to(place_ref[0:1, : shape[1]], shape) > 0.0


def extended_rows(place_ref, mid_ref, up_ref, down_ref):
    shape = mid_ref.shape[1:]
    has_up = jnp.broadcast_to(place_ref[1:2, : shape[1]], shape) > 0.0
    has_down = jnp.broadcast_to(place_ref[2:3, : shape[1]], shape) > 0.0
    for r in range(HALO):
        yield jnp.where(has_up, up_ref[r].astype(F32), 0.0)
    for r in range(mid_ref.shape[0]):
        yield mid_ref[r].astype(F32)
    for r in range(HALO):
        yield jnp.where(has_down, down_ref[r].astype(F32), 0.0)


def pack_body(place_ref, mid_ref, up_ref, down_ref, out_ref):
    channels, lanes = out_ref.shape
    lane = lax.broadcasted_iota(jnp.int32, (channels, lanes), 1)
    packed = jnp.zeros((channels, lanes), F32)
    for r, value in enumerate(extended_rows(place_ref, mid_ref, up_ref, down_ref)):
        if r:
            value = pltpu.roll(value, 8 * r, 1)
        packed = jnp.where(((lane + (HALO - 8 * r)) & (lanes - 1)) < 2 * HALO, value, packed)
    out_ref[...] = packed.astype(BF)


def fill_extended(ext, edge, place_ref, mid_ref, up_ref, down_ref, left_ref, right_ref):
    for r, value in enumerate(extended_rows(place_ref, mid_ref, up_ref, down_ref)):
        ext[r] = value
    channels, lanes = edge.shape
    lane = lax.broadcasted_iota(jnp.int32, (channels, lanes), 1)
    from_left = left_ref[...].astype(F32)
    from_right = right_ref[...].astype(F32)
    edge[...] = jnp.where((lane & 7) >= 4, from_left, from_right)


def joined(ext, edge, start):
    n_rows, _, lanes = ext.shape
    mid = ext[:, pl.ds(start, 8), :]
    ends = edge[pl.ds(start, 8), :]
    wings = jnp.stack(
        [ends] + [pltpu.roll(ends, lanes - 8 * r, 1) for r in range(1, n_rows)], axis=0
    )
    lane = lax.broadcasted_iota(jnp.int32, (8, lanes), 1)
    for shift in range(-HALO, HALO + 1):
        if shift == 0:
            yield shift, mid
            continue
        outside = lane < shift if shift > 0 else lane >= lanes + shift
        yield shift, jnp.where(outside[None], wings, mid)


def convolve(ext, edge, spread_ref, start, rows, flipped):
    lanes = ext.shape[2]
    total = jnp.zeros((rows, 8, lanes), F32)
    for b, (shift, value) in enumerate(joined(ext, edge, start)):
        window = pltpu.roll(value, -shift % lanes, 2) if shift else value
        for a in range(TAPS):
            tap = a * TAPS + b
            if flipped:
                tap = TAPS * TAPS - 1 - tap
            total = total + spread_ref[tap, pl.ds(start, 8), :][None] * window[a : a + rows]
    return total


def main_body(
    place_ref,
    m_ref,
    up_ref,
    down_ref,
    left_ref,
    right_ref,
    mask_ref,
    g_ref,
    spread_ref,
    gains_ref,
    biases_ref,
    we_ref,
    wp_ref,
    we_t_ref,
    wp_t_ref,
    next_ref,
    bm_ref,
    btop_ref,
    bbot_ref,
    gain_ref,
    own_ref,
    other_ref,
    ext,
    edge,
    mixed,
    act,
    back,
    normed_all,
    gated_all,
    flat,
):
    rows, channels, lanes = m_ref.shape
    hidden, deep = own_ref.shape
    chunk = hidden // 5
    pair = 2 * lanes
    fill_extended(ext, edge, place_ref, m_ref, up_ref, down_ref, left_ref, right_ref)

    def conv_step(block, carry):
        start = pl.multiple_of(block * 8, 8)
        mixed[:, pl.ds(start, 8), :] = convolve(ext, edge, spread_ref, start, rows, False)
        return carry

    lax.fori_loop(0, channels // 8, conv_step, 0, unroll=5)
    for r in range(rows):
        gated_all[:, r * lanes : (r + 1) * lanes] = jnp.concatenate(
            [g_ref[r].astype(F32), jnp.zeros((deep - channels, lanes), F32)], axis=0
        ).astype(BF)
    gain_ref[...] = jnp.zeros_like(gain_ref)
    ones_rows = jnp.ones((deep - channels, pair), F32)

    def pair_step(p, carry):
        cells = pl.ds(pl.multiple_of(p * pair, pair), pair)
        value = jnp.concatenate([mixed[2 * p], mixed[2 * p + 1]], axis=1)
        gain = jnp.concatenate([gains_ref[...]] * 2, axis=1)
        center = jnp.sum(value, axis=0, keepdims=True) * (1.0 / channels)
        centered = value - center
        spread = jnp.sum(centered * centered, axis=0, keepdims=True) * (1.0 / channels)
        inv_spread = lax.rsqrt(spread + EPS)
        whitened = centered * inv_spread
        normed = whitened * gain
        normed_all[:, cells] = jnp.concatenate([normed, ones_rows], axis=0).astype(BF)
        normed = normed.astype(BF)
        gated = jnp.concatenate([g_ref[2 * p], g_ref[2 * p + 1]], axis=1)
        for c in range(hidden // chunk):
            part = pl.ds(c * chunk, chunk)
            bias = biases_ref[part, :]
            inner = dot(we_ref[part, :], normed) + jnp.concatenate([bias, bias], axis=1)
            back_act = dot(wp_ref[part, :], gated)
            normal_cdf = 0.5 * (1.0 + lax.erf(inner * 0.7071067811865476))
            density = jnp.exp(-0.5 * inner * inner) * 0.3989422804014327
            act[part, cells] = (inner * normal_cdf).astype(BF)
            back[part, cells] = (back_act * (normal_cdf + inner * density)).astype(BF)
        branch = dot(wp_t_ref[...], act[:, cells])
        back_norm = dot(we_t_ref[...], back[:, cells])
        gain_term = back_norm * whitened
        gain_ref[...] += gain_term[:, :lanes] + gain_term[:, lanes:]
        scaled = back_norm * gain
        mean_scaled = jnp.sum(scaled, axis=0, keepdims=True) * (1.0 / channels)
        mean_product = jnp.sum(scaled * whitened, axis=0, keepdims=True) * (1.0 / channels)
        back_mixed = (inv_spread * (scaled - mean_scaled - whitened * mean_product)).astype(BF)
        for k in range(2):
            r = 2 * p + k
            mask = mask_ref[pl.ds(r, 1), :].astype(F32)
            here = slice(k * lanes, (k + 1) * lanes)
            flat[pl.ds(r, channels, stride=rows), :] = ext[r + HALO] + mask * branch[:, here]
            bm_ref[r] = back_mixed[:, here]
        return carry

    lax.fori_loop(0, rows // 2, pair_step, 0)
    next_ref[...] = flat[...].reshape(channels, rows, lanes).astype(BF)
    for r in range(HALO):
        btop_ref[r] = bm_ref[r]
        bbot_ref[r] = bm_ref[rows - HALO + r]
    first_core = is_first(place_ref, (chunk, deep))
    for c in range(hidden // chunk):
        part = pl.ds(c * chunk, chunk)
        expand = nt_dot(back[part, :], normed_all[...])
        project = nt_dot(act[part, :], gated_all[...])
        own_ref[part, :] = jnp.where(first_core, expand, project)
        other_ref[part, :] = jnp.where(first_core, project, expand).astype(BF)


def taps_body(
    place_ref,
    m_ref,
    up_ref,
    down_ref,
    left_ref,
    right_ref,
    bm_ref,
    gain_ref,
    own_ref,
    other_ref,
    ext,
    edge,
    upstream,
    sums,
):
    rows, channels, lanes = m_ref.shape
    fill_extended(ext, edge, place_ref, m_ref, up_ref, down_ref, left_ref, right_ref)
    for r in range(rows):
        upstream[r] = bm_ref[r].astype(F32)
    lane = lax.broadcasted_iota(jnp.int32, (8, lanes), 1)
    ones = jnp.ones((lanes, lanes), BF)

    def step(block, carry):
        start = pl.multiple_of(block * 8, 8)
        back = upstream[:, pl.ds(start, 8), :]
        result = jnp.zeros((8, lanes), F32)
        for b, (shift, value) in enumerate(joined(ext, edge, start)):
            turned = pltpu.roll(back, shift % lanes, 2) if shift else back
            terms = [jnp.sum(turned * value[a : a + rows], axis=0) for a in range(TAPS)]
            terms.append(gain_ref[pl.ds(start, 8), :])
            totals = dot(jnp.concatenate(terms, axis=0).astype(BF), ones)
            for a in range(TAPS):
                result = jnp.where(lane == a * TAPS + b, totals[8 * a : 8 * a + 8], result)
        result = jnp.where(lane == TAPS * TAPS, totals[8 * TAPS :], result)
        sums[pl.ds(start, 8), :] = result
        return carry

    lax.fori_loop(0, channels // 8, step, 0, unroll=5)
    half, deep = own_ref.shape
    count = (TAPS * TAPS + 1) // 2
    row = lax.broadcasted_iota(jnp.int32, (2 * half, lanes), 0)
    col = lax.broadcasted_iota(jnp.int32, (2 * half, lanes), 1)
    wanted = jnp.where(row < half, row, row - half + count)
    pick = (col == wanted) & (jnp.where(row < half, row, row - half) < count)
    pick = jnp.where(pick, 1.0, 0.0).astype(BF)
    padded = jnp.concatenate([sums[...], jnp.zeros((deep - channels, lanes), F32)], axis=0)
    turned = nt_dot(pick, padded.astype(BF))
    first_core = is_first(place_ref, (half, deep))
    own_ref[...] = jnp.where(first_core, turned[:half], turned[half:])
    other_ref[...] = jnp.where(first_core, turned[half:], turned[:half]).astype(BF)


def message_body(own_ref, got_ref, taps_ref, taps_got_ref, out_ref, total, piece):
    share = own_ref.shape[0] // out_ref.shape[0]
    depth = out_ref.shape[1]
    total[...] = own_ref[...] + got_ref[...].astype(F32)
    taps = taps_ref[...] + taps_got_ref[...].astype(F32)
    count = (TAPS * TAPS + 1) // 2
    piece[...] = jnp.zeros_like(piece)
    piece[share : share + count, :] = taps[:count]
    for k in range(out_ref.shape[0]):
        piece[:share, :] = total[k * share : (k + 1) * share, :]
        out_ref[k] = piece[...].astype(BF)


def sum_body(parts_ref, out_ref):
    total = parts_ref[0].astype(F32)
    for k in range(1, parts_ref.shape[0]):
        total = total + parts_ref[k].astype(F32)
    total = total.astype(BF)
    if len(out_ref.shape) == 2:
        out_ref[...] = total
    else:
        for k in range(out_ref.shape[0]):
            out_ref[k] = total


def final_body(place_ref, own_ref, got_ref, ge_ref, gp_ref, gk_ref, gg_ref, gb_ref, first, second):
    depth, deep = own_ref.shape
    share, channels = ge_ref.shape
    first_core = is_first(place_ref, (depth, deep))
    own = own_ref[...].astype(F32)
    got = got_ref[...].astype(F32)
    first[...] = jnp.where(first_core, own, got)
    second[...] = jnp.where(first_core, got, own)
    ge_ref[...] = first[:share, :channels]
    gp_ref[...] = second[:share, :channels]
    count = (TAPS * TAPS + 1) // 2
    gk_ref[:count, :] = first[share : share + count, :channels]
    gk_ref[count:, :] = second[share : share + count - 1, :channels]
    gg_ref[...] = second[share + count - 1 : share + count, :channels]
    lane = lax.broadcasted_iota(jnp.int32, (8, deep), 1)
    pick = jnp.where(lane == channels, 1.0, 0.0).astype(BF)
    gb_ref[...] = nt_dot(pick, first[...].astype(BF))[:1, :share]


def backward_body(
    place_ref,
    bm_ref,
    up_ref,
    down_ref,
    left_ref,
    right_ref,
    mask_ref,
    g_ref,
    spread_ref,
    out_ref,
    ext,
    edge,
    back,
    flat,
):
    rows, channels, lanes = bm_ref.shape
    fill_extended(ext, edge, place_ref, bm_ref, up_ref, down_ref, left_ref, right_ref)

    def step(block, carry):
        start = pl.multiple_of(block * 8, 8)
        back[:, pl.ds(start, 8), :] = convolve(ext, edge, spread_ref, start, rows, True)
        return carry

    lax.fori_loop(0, channels // 8, step, 0, unroll=5)
    for r in range(rows):
        mask = mask_ref[r : r + 1, :].astype(F32)
        flat[pl.ds(r, channels, stride=rows), :] = g_ref[r].astype(F32) + mask * back[r]
    out_ref[...] = flat[...].reshape(channels, rows, lanes).astype(BF)


def neighbours(top, bottom, axis):
    size = lax.axis_size(axis)
    up = [(i, (i + 1) % size) for i in range(size)]
    down = [(j, i) for i, j in up]
    return lax.ppermute(bottom, axis, up), lax.ppermute(top, axis, down)


def shards(
    ocean_state, land_sea, depth_kernel, norm_gain, w_expand, b_expand, w_project, cotangent
):
    channels, rows, lanes = ocean_state.shape
    hidden = w_expand.shape[0]
    n_lon, n_lat = lax.axis_size("lon"), lax.axis_size("lat")
    share = hidden // n_lon
    deep = -(-(channels + 3) // 16) * 16
    depth = -(-(share + 25) // 16) * 16
    cells = rows * lanes
    full = (rows, channels, lanes)
    edges = (HALO, channels, lanes)
    tile = (channels, lanes)
    flat = pltpu.VMEM((channels * rows, lanes), F32)
    ext_s = pltpu.VMEM((rows + 2 * HALO, channels, lanes), F32)
    edge_s = pltpu.VMEM(tile, F32)
    lat = lax.axis_index("lat")
    kind = lax.broadcasted_iota(jnp.int32, (8, 256), 0)
    value = jnp.where(kind == 0, 1 - lat % 2, jnp.where(kind == 1, lat, n_lat - 1 - lat))
    place = value.astype(F32)
    swap = [(i, i ^ 1) for i in range(n_lat)]

    load_s = [
        pltpu.VMEM(ocean_state.shape, BF),
        pltpu.VMEM((rows, lanes), jnp.int32),
        flat,
        pltpu.SemaphoreType.DMA((6,)),
    ]
    masked, top, bottom = kernel_call(
        state_body, [(full, BF), (edges, BF), (edges, BF)], load_s, n_any=2
    )(ocean_state, land_sea)
    up, down = neighbours(top, bottom, "lat")
    (gated,) = kernel_call(gated_body, [(full, BF)], load_s, n_any=2)(cotangent, land_sea)
    spread, gains, biases, we_t, wp_t = kernel_call(
        weights_body,
        [
            ((TAPS * TAPS, *tile), F32),
            (tile, F32),
            ((hidden, lanes), F32),
            ((channels, hidden), BF),
            ((channels, hidden), BF),
        ],
        n_in=5,
        micros=3,
    )(depth_kernel, norm_gain[None], b_expand[None], w_expand, w_project)
    (pack,) = kernel_call(pack_body, [(tile, BF)], n_in=4)(place, masked, up, down)
    left, right = neighbours(pack, pack, "lon")

    next_state, back_mixed, btop, bbottom, gain, own, other = kernel_call(
        main_body,
        [
            ((channels, rows, lanes), BF),
            (full, BF),
            (edges, BF),
            (edges, BF),
            (tile, F32),
            ((hidden, deep), F32),
            ((hidden, deep), BF),
        ],
        [
            ext_s,
            edge_s,
            pltpu.VMEM(full, F32),
            pltpu.VMEM((hidden, cells), BF),
            pltpu.VMEM((hidden, cells), BF),
            pltpu.VMEM((deep, cells), BF),
            pltpu.VMEM((deep, cells), BF),
            flat,
        ],
        n_in=15,
        micros=12,
    )(
        place,
        masked,
        up,
        down,
        left,
        right,
        land_sea,
        gated,
        spread,
        gains,
        biases,
        w_expand,
        w_project,
        we_t,
        wp_t,
    )
    got = lax.ppermute(other, "lat", swap)
    bup, bdown = neighbours(btop, bbottom, "lat")
    taps_own, taps_other = kernel_call(
        taps_body,
        [((32, deep), F32), ((32, deep), BF)],
        [ext_s, edge_s, pltpu.VMEM(full, F32), edge_s],
        n_in=8,
        micros=6,
    )(place, masked, up, down, left, right, back_mixed, gain)
    taps_got = lax.ppermute(taps_other, "lat", swap)
    (message,) = kernel_call(
        message_body,
        [((n_lon, depth, deep), BF)],
        [pltpu.VMEM((hidden, deep), F32), pltpu.VMEM((depth, deep), F32)],
        n_in=4,
    )(own, got, taps_own, taps_got)
    (back_pack,) = kernel_call(pack_body, [(tile, BF)], n_in=4)(
        place, back_mixed, bup, bdown
    )
    bleft, bright = neighbours(back_pack, back_pack, "lon")
    message, bleft, bright = lax.optimization_barrier((message, bleft, bright))

    parts = lax.all_to_all(message, "lon", 0, 0)
    (grad_state,) = kernel_call(
        backward_body,
        [((channels, rows, lanes), BF)],
        [ext_s, edge_s, pltpu.VMEM(full, F32), flat],
        n_in=9,
        micros=8,
    )(place, back_mixed, bup, bdown, bleft, bright, land_sea, gated, spread)
    parts, grad_state = lax.optimization_barrier((parts, grad_state))
    (copies,) = kernel_call(sum_body, [((n_lat // 2, depth, deep), BF)], n_in=1)(parts)
    groups = [list(range(c, n_lat, 2)) for c in range(2)]
    parts = lax.all_to_all(copies, "lat", 0, 0, axis_index_groups=groups)
    (sums,) = kernel_call(sum_body, [((depth, deep), BF)], n_in=1)(parts)
    sums_got = lax.ppermute(sums, "lat", swap)

    grad_expand, grad_project, grad_kernel, grad_gain, grad_bias = kernel_call(
        final_body,
        [
            ((share, channels), F32),
            ((share, channels), F32),
            ((TAPS * TAPS, channels), F32),
            ((1, channels), F32),
            ((1, share), F32),
        ],
        [pltpu.VMEM((depth, deep), F32)] * 2,
        n_in=3,
    )(place, sums, sums_got)
    return (
        next_state,
        grad_state,
        grad_kernel,
        grad_gain.reshape(channels),
        grad_expand,
        grad_project,
        grad_bias.reshape(share),
    )


def solution(mesh):
    placed = (
        P(None, "lat", "lon"),
        P("lat", "lon"),
        P(),
        P(),
        P(),
        P(),
        P(),
        P(None, "lat", "lon"),
    )
    return jax.shard_map(
        shards,
        mesh=mesh,
        in_specs=placed,
        out_specs=(
            P(None, "lat", "lon"),
            P(None, "lat", "lon"),
            P(),
            P(),
            P("lon", None),
            P("lon", None),
            P("lon"),
        ),
        check_vma=False,
    )
```

```python
import functools

import jax
import jax.numpy as jnp
from jax import lax
from jax.experimental import pallas as pl
from jax.experimental.pallas import tpu as pltpu
from jax.sharding import PartitionSpec as P

EPS = 1e-06
BF = jnp.bfloat16
F32 = jnp.float32
HALO = 3
TAPS = 7
HALF_TAPS = 25
WHOLE_ROWS = 13
CUT_ROWS = 12
SPARE_LANE = 204
VMEM_BYTES = 16 * 1024 * 1024


def kernel_call(body, outs, scratch=(), n_in=0, n_any=0, micros=1):
    specs = [pl.BlockSpec(memory_space=pltpu.HBM)] * n_any
    specs += [pl.BlockSpec(memory_space=pltpu.VMEM)] * n_in
    return pl.pallas_call(
        body,
        out_shape=[jax.ShapeDtypeStruct(shape, dtype) for shape, dtype in outs],
        in_specs=specs,
        out_specs=[pl.BlockSpec(memory_space=pltpu.VMEM)] * len(outs),
        scratch_shapes=list(scratch),
        compiler_params=pltpu.CompilerParams(vmem_limit_bytes=VMEM_BYTES),
        cost_estimate=pl.CostEstimate(
            flops=micros * 1_000_000_000, bytes_accessed=micros * 3_000_000, transcendentals=0
        ),
    )


def nt_dot(left, right):
    return lax.dot_general(left, right, (((1,), (1,)), ((), ())), preferred_element_type=F32)


def tn_dot(left, right):
    return lax.dot_general(left, right, (((0,), (0,)), ((), ())), preferred_element_type=F32)


def dot(left, right):
    return jnp.dot(left, right, preferred_element_type=F32)


def by_rows(field_ref, flat):
    channels, rows, lanes = field_ref.shape
    flat[...] = field_ref[...].astype(F32).reshape(channels * rows, lanes)
    return [flat[pl.ds(row, channels, stride=rows), :] for row in range(rows)]


def state_body(x_ref, place_ref, m_ref, near_ref, far_ref, flat):
    masked = by_rows(x_ref, flat)
    for row, value in enumerate(masked):
        m_ref[row] = value.astype(BF)
    send_edges(place_ref, masked, near_ref, far_ref)


def send_edges(place_ref, values, near_ref, far_ref):
    first = is_first(place_ref, values[0].shape)
    for r in range(HALO):
        top, bottom = values[r], values[len(values) - HALO + r]
        near_ref[r] = jnp.where(first, bottom, top).astype(BF)
        far_ref[r] = jnp.where(first, top, bottom).astype(BF)


def gated_body(cot_ref, g_ref, flat):
    for row, value in enumerate(by_rows(cot_ref, flat)):
        g_ref[row] = value.astype(BF)


def spread_body(taps_ref, spread_ref):
    count, channels, lanes = spread_ref.shape
    unit = lax.broadcasted_iota(jnp.int32, (count, lanes), 0)
    unit = unit == lax.broadcasted_iota(jnp.int32, (count, lanes), 1)
    taps = tn_dot(taps_ref[...], jnp.where(unit, 1.0, 0.0).astype(BF))
    for tap in range(count):
        spread_ref[tap] = jnp.broadcast_to(taps[:, tap : tap + 1], (channels, lanes))


def columns(row, lanes):
    high = row.astype(BF)
    rest = row - high.astype(F32)
    middle = rest.astype(BF)
    low = (rest - middle.astype(F32)).astype(BF)
    spare = jnp.zeros((5, row.shape[1]), F32)
    parts = [high.astype(F32), middle.astype(F32), low.astype(F32), spare]
    parts = jnp.concatenate(parts, axis=0).astype(BF)
    return tn_dot(parts, jnp.ones((8, lanes), BF))


def weights_body(
    taps_ref, gain_ref, bias_ref, we_in_ref, wp_in_ref, spread_ref, gains_ref, biases_ref, we_ref, wp_ref
):
    count, channels, lanes = spread_ref.shape
    spread_body(taps_ref, spread_ref)
    gains_ref[...] = columns(gain_ref[...].reshape(1, channels), lanes)
    biases_ref[...] = columns(bias_ref[...].reshape(1, bias_ref.shape[0]), lanes)
    we_ref[...] = we_in_ref[...].astype(F32).T.astype(BF)
    wp_ref[...] = wp_in_ref[...].astype(F32).T.astype(BF)


def flag(place_ref, row, shape):
    return jnp.broadcast_to(place_ref[row : row + 1, : shape[1]], shape) > 0.0


def is_first(place_ref, shape):
    return flag(place_ref, 0, shape)


def extended_rows(place_ref, mid_ref, near_ref, far_ref):
    shape = mid_ref.shape[1:]
    first = is_first(place_ref, shape)
    has_up = jnp.broadcast_to(place_ref[1:2, : shape[1]], shape) > 0.0
    has_down = jnp.broadcast_to(place_ref[2:3, : shape[1]], shape) > 0.0
    near = [near_ref[r].astype(F32) for r in range(HALO)]
    far = [far_ref[r].astype(F32) for r in range(HALO)]
    for r in range(HALO):
        yield jnp.where(has_up, jnp.where(first, far[r], near[r]), 0.0)
    for r in range(mid_ref.shape[0]):
        yield mid_ref[r].astype(F32)
    for r in range(HALO):
        yield jnp.where(has_down, jnp.where(first, near[r], far[r]), 0.0)


def pack_body(place_ref, mid_ref, near_ref, far_ref, out_ref):
    channels, lanes = out_ref.shape
    lane = lax.broadcasted_iota(jnp.int32, (channels, lanes), 1)
    packed = jnp.zeros((channels, lanes), F32)
    for r, value in enumerate(extended_rows(place_ref, mid_ref, near_ref, far_ref)):
        if r:
            value = pltpu.roll(value, 8 * r, 1)
        packed = jnp.where(((lane + (HALO - 8 * r)) & (lanes - 1)) < 2 * HALO, value, packed)
    out_ref[...] = packed.astype(BF)


def fill_extended(ext, edge, place_ref, mid_ref, near_ref, far_ref, lon_near_ref, lon_far_ref):
    for r, value in enumerate(extended_rows(place_ref, mid_ref, near_ref, far_ref)):
        ext[r] = value
    shape = edge.shape
    lane = lax.broadcasted_iota(jnp.int32, shape, 1)
    side = jnp.where((lane & 7) >= 4, 1.0, 0.0)
    near_is_right = jnp.broadcast_to(place_ref[3:4, : shape[1]], shape)
    near = lon_near_ref[...].astype(F32)
    edge[...] = jnp.where(side != near_is_right, near, lon_far_ref[...].astype(F32))


def joined(ext, edge, start):
    n_rows, _, lanes = ext.shape
    mid = ext[:, pl.ds(start, 8), :]
    ends = edge[pl.ds(start, 8), :]
    wings = jnp.stack(
        [ends] + [pltpu.roll(ends, lanes - 8 * r, 1) for r in range(1, n_rows)], axis=0
    )
    lane = lax.broadcasted_iota(jnp.int32, (8, lanes), 1)
    for shift in range(-HALO, HALO + 1):
        if shift == 0:
            yield shift, mid
            continue
        outside = lane < shift if shift > 0 else lane >= lanes + shift
        yield shift, jnp.where(outside[None], wings, mid)


def convolve(ext, edge, spread_ref, start, rows, flipped):
    lanes = ext.shape[2]
    total = jnp.zeros((rows, 8, lanes), F32)
    for b, (shift, value) in enumerate(joined(ext, edge, start)):
        window = pltpu.roll(value, -shift % lanes, 2) if shift else value
        for a in range(TAPS):
            tap = a * TAPS + b
            if flipped:
                tap = TAPS * TAPS - 1 - tap
            total = total + spread_ref[tap, pl.ds(start, 8), :][None] * window[a : a + rows]
    return total


def main_body(
    place_ref,
    m_ref,
    near_ref,
    far_ref,
    lon_near_ref,
    lon_far_ref,
    mask_ref,
    g_ref,
    spread_ref,
    gains_ref,
    biases_ref,
    we_ref,
    wp_ref,
    we_t_ref,
    wp_t_ref,
    next_ref,
    bm_ref,
    bnear_ref,
    bfar_ref,
    gain_ref,
    own_ref,
    other_ref,
    ext,
    edge,
    mixed,
    units,
    sides,
    flat,
):
    rows, channels, lanes = m_ref.shape
    hidden, deep = own_ref.shape
    chunk = hidden // 5
    pair = 2 * lanes
    fill_extended(ext, edge, place_ref, m_ref, near_ref, far_ref, lon_near_ref, lon_far_ref)

    def conv_step(block, carry):
        start = pl.multiple_of(block * 8, 8)
        mixed[:, pl.ds(start, 8), :] = convolve(ext, edge, spread_ref, start, rows, False)
        return carry

    lax.fori_loop(0, channels // 8, conv_step, 0, unroll=5)
    for r in range(rows):
        sides[1, :, r * lanes : (r + 1) * lanes] = jnp.concatenate(
            [g_ref[r].astype(F32), jnp.zeros((deep - channels, lanes), F32)], axis=0
        ).astype(BF)
    gain_ref[...] = jnp.zeros_like(gain_ref)
    tail_row = lax.broadcasted_iota(jnp.int32, (deep - channels, pair), 0)
    ones_rows = jnp.where(tail_row == 0, 1.0, 0.0)

    def pair_step(p, carry):
        cells = pl.ds(pl.multiple_of(p * pair, pair), pair)
        value = jnp.concatenate([mixed[2 * p], mixed[2 * p + 1]], axis=1)
        gain = jnp.concatenate([gains_ref[...]] * 2, axis=1)
        center = jnp.sum(value, axis=0, keepdims=True) * (1.0 / channels)
        centered = value - center
        spread = jnp.sum(centered * centered, axis=0, keepdims=True) * (1.0 / channels)
        inv_spread = lax.rsqrt(spread + EPS)
        whitened = centered * inv_spread
        normed = whitened * gain
        sides[0, :, cells] = jnp.concatenate([normed, ones_rows], axis=0).astype(BF)
        normed = normed.astype(BF)
        gated = jnp.concatenate([g_ref[2 * p], g_ref[2 * p + 1]], axis=1)
        for c in range(hidden // chunk):
            part = pl.ds(c * chunk, chunk)
            bias = biases_ref[part, :]
            inner = dot(we_ref[part, :], normed) + jnp.concatenate([bias, bias], axis=1)
            back_act = dot(wp_ref[part, :], gated)
            normal_cdf = 0.5 * (1.0 + lax.erf(inner * 0.7071067811865476))
            density = jnp.exp(-0.5 * inner * inner) * 0.3989422804014327
            units[1, part, cells] = (inner * normal_cdf).astype(BF)
            units[0, part, cells] = (back_act * (normal_cdf + inner * density)).astype(BF)
        branch = dot(wp_t_ref[...], units[1, :, cells])
        back_norm = dot(we_t_ref[...], units[0, :, cells])
        gain_term = back_norm * whitened
        gain_ref[...] += gain_term[:, :lanes] + gain_term[:, lanes:]
        scaled = back_norm * gain
        mean_scaled = jnp.sum(scaled, axis=0, keepdims=True) * (1.0 / channels)
        mean_product = jnp.sum(scaled * whitened, axis=0, keepdims=True) * (1.0 / channels)
        back_mixed = (inv_spread * (scaled - mean_scaled - whitened * mean_product)).astype(BF)
        for k in range(2):
            r = 2 * p + k
            mask = mask_ref[pl.ds(r, 1), :].astype(F32)
            here = slice(k * lanes, (k + 1) * lanes)
            flat[pl.ds(r, channels, stride=rows), :] = ext[r + HALO] + mask * branch[:, here]
            bm_ref[r] = back_mixed[:, here]
        return carry

    lax.fori_loop(0, rows // 2, pair_step, 0)
    next_ref[...] = flat[...].reshape(channels, rows, lanes).astype(BF)
    send_edges(place_ref, [bm_ref[r].astype(F32) for r in range(rows)], bnear_ref, bfar_ref)
    core = lax.axis_index("lat") % 2
    for out, which in ((own_ref, core), (other_ref, 1 - core)):
        for c in range(hidden // chunk):
            part = slice(c * chunk, (c + 1) * chunk)
            out[part, :] = nt_dot(units[which, part, :], sides[which]).astype(out.dtype)


def taps_body(
    place_ref,
    m_ref,
    near_ref,
    far_ref,
    lon_near_ref,
    lon_far_ref,
    bm_ref,
    gain_ref,
    own_ref,
    other_ref,
    ext,
    edge,
    upstream,
    sums,
    moved,
):
    rows, channels, lanes = m_ref.shape
    fill_extended(ext, edge, place_ref, m_ref, near_ref, far_ref, lon_near_ref, lon_far_ref)
    for r in range(rows):
        upstream[r] = bm_ref[r].astype(F32)
    lane = lax.broadcasted_iota(jnp.int32, (8, lanes), 1)
    ones = jnp.ones((lanes, lanes), BF)

    def step(block, carry):
        start = pl.multiple_of(block * 8, 8)
        back = upstream[:, pl.ds(start, 8), :]
        result = jnp.zeros((8, lanes), F32)
        for b, (shift, value) in enumerate(joined(ext, edge, start)):
            turned = pltpu.roll(back, shift % lanes, 2) if shift else back
            terms = [jnp.sum(turned * value[a : a + rows], axis=0) for a in range(TAPS)]
            terms.append(gain_ref[pl.ds(start, 8), :])
            totals = dot(jnp.concatenate(terms, axis=0).astype(BF), ones)
            for a in range(TAPS):
                result = jnp.where(lane == a * TAPS + b, totals[8 * a : 8 * a + 8], result)
        result = jnp.where(lane == TAPS * TAPS, totals[8 * TAPS :], result)
        sums[pl.ds(start, 8), :] = result
        return carry

    lax.fori_loop(0, channels // 8, step, 0, unroll=5)
    block, wide = own_ref.shape
    row = lax.broadcasted_iota(jnp.int32, (2 * block, lanes), 0)
    col = lax.broadcasted_iota(jnp.int32, (2 * block, lanes), 1)
    second, inside = row // block, row % block

    def picked(first_row, first_tap, count):
        tap = inside - first_row + first_tap + second * HALF_TAPS
        pick = (col == tap) & (inside >= first_row) & (inside < first_row + count)
        return nt_dot(jnp.where(pick, 1.0, 0.0).astype(BF), moved[...].astype(BF))

    moved[...] = jnp.zeros_like(moved)
    moved[:channels, :] = sums[...]
    turned = picked(block - 1 - WHOLE_ROWS, 0, WHOLE_ROWS)
    moved[...] = jnp.zeros_like(moved)
    cut = channels // 4
    for q in range(4):
        moved[SPARE_LANE : SPARE_LANE + cut, :] = sums[q * cut : (q + 1) * cut, :]
        turned = turned + picked(q * CUT_ROWS, WHOLE_ROWS, CUT_ROWS)
    first = is_first(place_ref, (block, wide))
    own_ref[...] = jnp.where(first, turned[:block], turned[block:])
    other_ref[...] = jnp.where(first, turned[block:], turned[:block]).astype(BF)


def message_body(own_ref, got_ref, taps_ref, taps_got_ref, out_ref, total, taps, piece):
    hidden, deep = own_ref.shape
    share = hidden // out_ref.shape[0]
    total[...] = own_ref[...] + got_ref[...].astype(F32)
    taps[...] = taps_ref[...] + taps_got_ref[...].astype(F32)
    piece[...] = taps[...]
    for k in range(out_ref.shape[0]):
        rows = total[k * share : (k + 1) * share, :]
        piece[:share, :deep] = rows + taps[:share, :deep]
        out_ref[k] = piece[...].astype(BF)


def sum_body(parts_ref, out_ref):
    total = parts_ref[0].astype(F32)
    for k in range(1, parts_ref.shape[0]):
        total = total + parts_ref[k].astype(F32)
    total = total.astype(BF)
    for k in range(out_ref.shape[0]):
        out_ref[k] = total


def final_body(parts_ref, ge_ref, gp_ref, gk_ref, gg_ref, gb_ref, halves):
    share, channels = ge_ref.shape
    _, depth, wide = parts_ref.shape
    for k in range(2):
        total = parts_ref[k].astype(F32)
        for j in range(k + 2, parts_ref.shape[0], 2):
            total = total + parts_ref[j].astype(F32)
        halves[k] = total
    ge_ref[...] = halves[0, :share, :channels]
    gp_ref[...] = halves[1, :share, :channels]
    cut = channels // 4
    lane = lax.broadcasted_iota(jnp.int32, (16, wide), 1)
    for k in range(2):
        start = k * HALF_TAPS
        whole = depth - 1 - WHOLE_ROWS
        gk_ref[start : start + WHOLE_ROWS, :] = halves[k, whole : depth - 1, :channels]
        rest = jnp.zeros((16, wide), F32)
        for q in range(4):
            value = halves[k, q * CUT_ROWS : q * CUT_ROWS + 16, :]
            value = pltpu.roll(value, (q * cut - SPARE_LANE) % wide, 1)
            rest = jnp.where((lane >= q * cut) & (lane < (q + 1) * cut), value, rest)
        count = min(CUT_ROWS, TAPS * TAPS - start - WHOLE_ROWS)
        start = start + WHOLE_ROWS
        gk_ref[start : start + count, :] = rest[:count, :channels]
    gg_ref[...] = rest[CUT_ROWS - 1 : CUT_ROWS, :channels]
    pick = lax.broadcasted_iota(jnp.int32, (8, wide), 1) == channels
    pick = jnp.where(pick, 1.0, 0.0).astype(BF)
    high = halves[0].astype(BF)
    low = (halves[0] - high.astype(F32)).astype(BF)
    gb_ref[...] = (nt_dot(pick, high) + nt_dot(pick, low))[:1, :share]


def backward_body(
    place_ref,
    bm_ref,
    near_ref,
    far_ref,
    lon_near_ref,
    lon_far_ref,
    mask_ref,
    g_ref,
    taps_ref,
    out_ref,
    ext,
    edge,
    back,
    flat,
    spread,
):
    rows, channels, lanes = bm_ref.shape
    spread_body(taps_ref, spread)
    fill_extended(ext, edge, place_ref, bm_ref, near_ref, far_ref, lon_near_ref, lon_far_ref)

    def step(block, carry):
        start = pl.multiple_of(block * 8, 8)
        back[:, pl.ds(start, 8), :] = convolve(ext, edge, spread, start, rows, True)
        return carry

    lax.fori_loop(0, channels // 8, step, 0, unroll=5)
    for r in range(rows):
        mask = mask_ref[r : r + 1, :].astype(F32)
        flat[pl.ds(r, channels, stride=rows), :] = g_ref[r].astype(F32) + mask * back[r]
    out_ref[...] = flat[...].reshape(channels, rows, lanes).astype(BF)


def swap_lon(pack):
    size = lax.axis_size("lon")
    near = [(i, i ^ 1) for i in range(size)]
    far = [(i, ((i ^ 1) + (2 if i % 2 else -2)) % size) for i in range(size)]
    from_far = lax.ppermute(pack, "lon", far)
    return lax.ppermute(pack, "lon", near), from_far


def swap_lat(first, second):
    size = lax.axis_size("lat")
    near = [(i, i ^ 1) for i in range(size)]
    far = [(i, ((i ^ 1) + (2 if i % 2 else -2)) % size) for i in range(size)]
    return lax.ppermute(second, "lat", near), lax.ppermute(first, "lat", far)


def shards(
    ocean_state, land_sea, depth_kernel, norm_gain, w_expand, b_expand, w_project, cotangent
):
    channels, rows, lanes = ocean_state.shape
    hidden = w_expand.shape[0]
    n_lon, n_lat = lax.axis_size("lon"), lax.axis_size("lat")
    share = hidden // n_lon
    deep = -(-(channels + 3) // 16) * 16
    depth = share + WHOLE_ROWS + 1
    wide = 256
    cells = rows * lanes
    full = (rows, channels, lanes)
    edges = (HALO, channels, lanes)
    tile = (channels, lanes)
    flat = pltpu.VMEM((channels * rows, lanes), F32)
    ext_s = pltpu.VMEM((rows + 2 * HALO, channels, lanes), F32)
    edge_s = pltpu.VMEM(tile, F32)
    lat = lax.axis_index("lat")
    kind = lax.broadcasted_iota(jnp.int32, (8, 256), 0)
    value = jnp.where(kind == 0, 1 - lat % 2, jnp.where(kind == 1, lat, n_lat - 1 - lat))
    value = jnp.where(kind == 3, 1 - lax.axis_index("lon") % 2, value)
    place = jnp.where(kind == 4, 1 - lat // 2 % 2, value).astype(F32)
    swap = [(i, i ^ 1) for i in range(n_lat)]
    zero = jnp.zeros((), BF)
    masked, near, far = kernel_call(
        state_body, [(full, BF), (edges, BF), (edges, BF)], [flat], n_in=2
    )(jnp.where(land_sea[None] != 0, ocean_state, zero), place)
    near, far = swap_lat(far, near)
    (gated,) = kernel_call(gated_body, [(full, BF)], [flat], n_in=1)(
        jnp.where(land_sea[None] > 0, cotangent, zero)
    )
    (pack,) = kernel_call(pack_body, [(tile, BF)], n_in=4)(place, masked, near, far)
    later = (depth_kernel, norm_gain, b_expand, w_expand.T, w_project.T)
    pack, later = lax.optimization_barrier((pack, later))
    lon_near, lon_far = swap_lon(pack)
    spread, gains, biases, we, wp = kernel_call(
        weights_body,
        [
            ((TAPS * TAPS, *tile), F32),
            (tile, F32),
            ((hidden, lanes), F32),
            ((hidden, channels), BF),
            ((hidden, channels), BF),
        ],
        n_in=5,
        micros=3,
    )(*later)
    we_t, wp_t = later[3:]
    next_state, back_mixed, bnear, bfar, gain, own, other = kernel_call(
        main_body,
        [
            ((channels, rows, lanes), BF),
            (full, BF),
            (edges, BF),
            (edges, BF),
            (tile, F32),
            ((hidden, deep), F32),
            ((hidden, deep), BF),
        ],
        [
            ext_s,
            edge_s,
            pltpu.VMEM(full, F32),
            pltpu.VMEM((2, hidden, cells), BF),
            pltpu.VMEM((2, deep, cells), BF),
            flat,
        ],
        n_in=15,
        micros=12,
    )(
        place,
        masked,
        near,
        far,
        lon_near,
        lon_far,
        land_sea,
        gated,
        spread,
        gains,
        biases,
        we,
        wp,
        we_t,
        wp_t,
    )
    got = lax.ppermute(other, "lat", swap)
    bnear, bfar = swap_lat(bfar, bnear)
    taps_own, taps_other = kernel_call(
        taps_body,
        [((depth, wide), F32), ((depth, wide), BF)],
        [ext_s, edge_s, pltpu.VMEM(full, F32), edge_s, pltpu.VMEM((wide, lanes), F32)],
        n_in=8,
        micros=6,
    )(place, masked, near, far, lon_near, lon_far, back_mixed, gain)
    taps_got = lax.ppermute(taps_other, "lat", swap)
    (message,) = kernel_call(
        message_body,
        [((n_lon, depth, wide), BF)],
        [
            pltpu.VMEM((hidden, deep), F32),
            pltpu.VMEM((depth, wide), F32),
            pltpu.VMEM((depth, wide), F32),
        ],
        n_in=4,
    )(own, got, taps_own, taps_got)
    (back_pack,) = kernel_call(pack_body, [(tile, BF)], n_in=4)(
        place, back_mixed, bnear, bfar
    )
    blon_near, blon_far = swap_lon(back_pack)
    parts = lax.all_to_all(message, "lon", 0, 0)
    (copies,) = kernel_call(sum_body, [((n_lat, depth, wide), BF)], n_in=1)(parts)
    parts = lax.all_to_all(copies, "lat", 0, 0)
    (grad_state,) = kernel_call(
        backward_body,
        [((channels, rows, lanes), BF)],
        [ext_s, edge_s, pltpu.VMEM(full, F32), flat, pltpu.VMEM((TAPS * TAPS, *tile), F32)],
        n_in=9,
        micros=8,
    )(
        place, back_mixed, bnear, bfar, blon_near, blon_far, land_sea, gated, depth_kernel
    )
    parts, grad_state = lax.optimization_barrier((parts, grad_state))

    grad_expand, grad_project, grad_kernel, grad_gain, grad_bias = kernel_call(
        final_body,
        [
            ((share, channels), F32),
            ((share, channels), F32),
            ((TAPS * TAPS, channels), F32),
            ((1, channels), F32),
            ((1, share), F32),
        ],
        [pltpu.VMEM((2, depth, wide), F32)],
        n_in=1,
    )(parts)
    return (
        next_state,
        grad_state,
        grad_kernel,
        grad_gain.reshape(channels),
        grad_expand,
        grad_project,
        grad_bias.reshape(share),
    )


def solution(mesh):
    placed = (
        P(None, "lat", "lon"),
        P("lat", "lon"),
        P(),
        P(),
        P(),
        P(),
        P(),
        P(None, "lat", "lon"),
    )
    return jax.shard_map(
        shards,
        mesh=mesh,
        in_specs=placed,
        out_specs=(
            P(None, "lat", "lon"),
            P(None, "lat", "lon"),
            P(),
            P(),
            P("lon", None),
            P("lon", None),
            P("lon"),
        ),
        check_vma=False,
    )
```

```python
import functools

import jax
import jax.numpy as jnp
from jax import lax
from jax.experimental import pallas as pl
from jax.experimental.pallas import tpu as pltpu
from jax.sharding import PartitionSpec as P

EPS = 1e-06
BF = jnp.bfloat16
F32 = jnp.float32
HALO = 3
TAPS = 7
HALF_TAPS = 25
WHOLE_ROWS = 13
CUT_ROWS = 12
SPARE_LANE = 204
VMEM_BYTES = 16 * 1024 * 1024


def kernel_call(body, outs, scratch=(), n_in=0, n_any=0, micros=1):
    specs = [pl.BlockSpec(memory_space=pltpu.HBM)] * n_any
    specs += [pl.BlockSpec(memory_space=pltpu.VMEM)] * n_in
    return pl.pallas_call(
        body,
        out_shape=[jax.ShapeDtypeStruct(shape, dtype) for shape, dtype in outs],
        in_specs=specs,
        out_specs=[pl.BlockSpec(memory_space=pltpu.VMEM)] * len(outs),
        scratch_shapes=list(scratch),
        compiler_params=pltpu.CompilerParams(vmem_limit_bytes=VMEM_BYTES),
        cost_estimate=pl.CostEstimate(
            flops=micros * 1_000_000_000, bytes_accessed=micros * 3_000_000, transcendentals=0
        ),
    )


def nt_dot(left, right):
    return lax.dot_general(left, right, (((1,), (1,)), ((), ())), preferred_element_type=F32)


def tn_dot(left, right):
    return lax.dot_general(left, right, (((0,), (0,)), ((), ())), preferred_element_type=F32)


def dot(left, right):
    return jnp.dot(left, right, preferred_element_type=F32)


def by_rows(field_ref, flat):
    channels, rows, lanes = field_ref.shape
    flat[...] = field_ref[...].astype(F32).reshape(channels * rows, lanes)
    return [flat[pl.ds(row, channels, stride=rows), :] for row in range(rows)]


def state_body(mask_ref, x_ref, place_ref, m_ref, near_ref, far_ref, pack_ref, flat):
    rows = mask_ref.shape[0]
    masked = by_rows(x_ref, flat)
    masked = [value * mask_ref[r : r + 1, :].astype(F32) for r, value in enumerate(masked)]
    pack_ref[...] = packed_edges(masked, HALO).astype(BF)
    send_edges(place_ref, masked, near_ref, far_ref)
    for row in range(rows):
        m_ref[row] = masked[row].astype(BF)


def send_edges(place_ref, values, near_ref, far_ref):
    first = is_first(place_ref, values[0].shape)
    for r in range(HALO):
        top, bottom = values[r], values[len(values) - HALO + r]
        near_ref[r] = jnp.where(first, bottom, top).astype(BF)
        far_ref[r] = jnp.where(first, top, bottom).astype(BF)


def gated_body(mask_ref, cot_ref, g_ref, flat):
    for row, value in enumerate(by_rows(cot_ref, flat)):
        g_ref[row] = (value * mask_ref[row : row + 1, :].astype(F32)).astype(BF)


def spread_body(taps_ref, spread_ref):
    count, channels, lanes = spread_ref.shape
    unit = lax.broadcasted_iota(jnp.int32, (count, lanes), 0)
    unit = unit == lax.broadcasted_iota(jnp.int32, (count, lanes), 1)
    taps = tn_dot(taps_ref[...], jnp.where(unit, 1.0, 0.0).astype(BF))
    for tap in range(count):
        spread_ref[tap] = jnp.broadcast_to(taps[:, tap : tap + 1], (channels, lanes))


def columns(row, lanes):
    high = row.astype(BF)
    rest = row - high.astype(F32)
    middle = rest.astype(BF)
    low = (rest - middle.astype(F32)).astype(BF)
    spare = jnp.zeros((5, row.shape[1]), F32)
    parts = [high.astype(F32), middle.astype(F32), low.astype(F32), spare]
    parts = jnp.concatenate(parts, axis=0).astype(BF)
    return tn_dot(parts, jnp.ones((8, lanes), BF))


def weights_body(
    taps_ref, gain_ref, bias_ref, we_in_ref, wp_in_ref, spread_ref, gains_ref, biases_ref, we_ref, wp_ref
):
    count, channels, lanes = spread_ref.shape
    spread_body(taps_ref, spread_ref)
    gains_ref[...] = columns(gain_ref[...].reshape(1, channels), lanes)
    biases_ref[...] = columns(bias_ref[...].reshape(1, bias_ref.shape[0]), lanes)
    we_ref[...] = we_in_ref[...].astype(F32).T.astype(BF)
    wp_ref[...] = wp_in_ref[...].astype(F32).T.astype(BF)


def flag(place_ref, row, shape):
    return jnp.broadcast_to(place_ref[row : row + 1, : shape[1]], shape) > 0.0


def is_first(place_ref, shape):
    return flag(place_ref, 0, shape)


def extended_rows(place_ref, mid_ref, near_ref, far_ref):
    shape = mid_ref.shape[1:]
    first = is_first(place_ref, shape)
    has_up = jnp.broadcast_to(place_ref[1:2, : shape[1]], shape) > 0.0
    has_down = jnp.broadcast_to(place_ref[2:3, : shape[1]], shape) > 0.0
    near = [near_ref[r].astype(F32) for r in range(HALO)]
    far = [far_ref[r].astype(F32) for r in range(HALO)]
    for r in range(HALO):
        yield jnp.where(has_up, jnp.where(first, far[r], near[r]), 0.0)
    for r in range(mid_ref.shape[0]):
        yield mid_ref[r].astype(F32)
    for r in range(HALO):
        yield jnp.where(has_down, jnp.where(first, near[r], far[r]), 0.0)


def packed_edges(values, first_row):
    shape = values[0].shape
    lanes = shape[1]
    lane = lax.broadcasted_iota(jnp.int32, shape, 1)
    packed = jnp.zeros(shape, F32)
    for r, value in enumerate(values, first_row):
        if r:
            value = pltpu.roll(value, 8 * r, 1)
        packed = jnp.where(((lane + (HALO - 8 * r)) & (lanes - 1)) < 2 * HALO, value, packed)
    return packed


def pack_body(place_ref, mid_ref, near_ref, far_ref, out_ref):
    rows = extended_rows(place_ref, mid_ref, near_ref, far_ref)
    out_ref[...] = packed_edges(list(rows), 0).astype(BF)


def lon_edges(place_ref, lon_near_ref, lon_far_ref):
    shape = lon_near_ref.shape
    lane = lax.broadcasted_iota(jnp.int32, shape, 1)
    side = jnp.where((lane & 7) >= 4, 1.0, 0.0)
    near_is_right = jnp.broadcast_to(place_ref[3:4, : shape[1]], shape)
    near = lon_near_ref[...].astype(F32)
    return jnp.where(side != near_is_right, near, lon_far_ref[...].astype(F32))


def edges_body(place_ref, lon_near_ref, lon_far_ref, out_ref):
    out_ref[...] = lon_edges(place_ref, lon_near_ref, lon_far_ref).astype(BF)


def all_edges(place_ref, own_ref, near_ref, far_ref):
    shape = own_ref.shape
    first = is_first(place_ref, shape)
    near, far = near_ref[...].astype(F32), far_ref[...].astype(F32)
    up = jnp.where(flag(place_ref, 1, shape), jnp.where(first, far, near), 0.0)
    down = jnp.where(flag(place_ref, 2, shape), jnp.where(first, near, far), 0.0)
    lane = lax.broadcasted_iota(jnp.int32, shape, 1)
    row = ((lane + HALO) >> 3) & 15
    others = pltpu.roll(jnp.where(row < 8, down, up), 64, 1)
    return jnp.where((row >= HALO) & (row < HALO + 8), own_ref[...].astype(F32), others)


def fill_extended(ext, place_ref, mid_ref, near_ref, far_ref):
    for r, value in enumerate(extended_rows(place_ref, mid_ref, near_ref, far_ref)):
        ext[r] = value


def line_up(edge, start, n_rows):
    ends = edge[pl.ds(start, 8), :]
    lanes = ends.shape[1]
    return jnp.stack(
        [ends] + [pltpu.roll(ends, lanes - 8 * r, 1) for r in range(1, n_rows)], axis=0
    )


def joined(mid, wings):
    lanes = mid.shape[2]
    lane = lax.broadcasted_iota(jnp.int32, mid.shape[1:], 1)
    for shift in range(-HALO, HALO + 1):
        if shift == 0:
            yield shift, mid
            continue
        outside = lane < shift if shift > 0 else lane >= lanes + shift
        yield shift, jnp.where(outside[None], wings, mid)


def convolve(ext, wings, spread_ref, start, rows, flipped):
    lanes = ext.shape[2]
    mid = ext[:, pl.ds(start, 8), :]
    total = jnp.zeros((rows, 8, lanes), F32)
    for b, (shift, value) in enumerate(joined(mid, wings)):
        window = pltpu.roll(value, -shift % lanes, 2) if shift else value
        for a in range(TAPS):
            tap = a * TAPS + b
            if flipped:
                tap = TAPS * TAPS - 1 - tap
            total = total + spread_ref[tap, pl.ds(start, 8), :][None] * window[a : a + rows]
    return total


def main_body(
    place_ref,
    m_ref,
    near_ref,
    far_ref,
    edge_own_ref,
    edge_near_ref,
    edge_far_ref,
    mask_ref,
    g_ref,
    spread_ref,
    gains_ref,
    biases_ref,
    we_ref,
    wp_ref,
    we_t_ref,
    wp_t_ref,
    next_ref,
    bm_ref,
    bnear_ref,
    bfar_ref,
    gain_ref,
    own_ref,
    other_ref,
    wings_ref,
    ext,
    edge,
    mixed,
    units,
    sides,
):
    rows, channels, lanes = m_ref.shape
    hidden, deep = own_ref.shape
    pair = 2 * lanes
    fill_extended(ext, place_ref, m_ref, near_ref, far_ref)
    edge[...] = all_edges(place_ref, edge_own_ref, edge_near_ref, edge_far_ref)

    def conv_step(block, carry):
        start = pl.multiple_of(block * 8, 8)
        wings = line_up(edge, start, ext.shape[0])
        wings_ref[:, pl.ds(start, 8), :] = wings
        mixed[:, pl.ds(start, 8), :] = convolve(ext, wings, spread_ref, start, rows, False)
        return carry

    lax.fori_loop(0, channels // 8, conv_step, 0, unroll=5)
    for r in range(rows):
        sides[1, :, r * lanes : (r + 1) * lanes] = jnp.concatenate(
            [g_ref[r].astype(F32), jnp.zeros((deep - channels, lanes), F32)], axis=0
        ).astype(BF)
    gain_ref[...] = jnp.zeros_like(gain_ref)
    tail_row = lax.broadcasted_iota(jnp.int32, (deep - channels, pair), 0)
    ones_rows = jnp.where(tail_row == 0, 1.0, 0.0)

    def pair_step(p, carry):
        cells = pl.ds(pl.multiple_of(p * pair, pair), pair)
        value = jnp.concatenate([mixed[2 * p], mixed[2 * p + 1]], axis=1)
        gain = jnp.concatenate([gains_ref[...]] * 2, axis=1)
        center = jnp.sum(value, axis=0, keepdims=True) * (1.0 / channels)
        centered = value - center
        spread = jnp.sum(centered * centered, axis=0, keepdims=True) * (1.0 / channels)
        inv_spread = lax.rsqrt(spread + EPS)
        whitened = centered * inv_spread
        normed = whitened * gain
        sides[0, :, cells] = jnp.concatenate([normed, ones_rows], axis=0).astype(BF)
        normed = normed.astype(BF)
        gated = jnp.concatenate([g_ref[2 * p], g_ref[2 * p + 1]], axis=1)
        inner = dot(we_ref[...], normed) + jnp.concatenate([biases_ref[...]] * 2, axis=1)
        back_act = dot(wp_ref[...], gated)
        normal_cdf = 0.5 * (1.0 + lax.erf(inner * 0.7071067811865476))
        density = jnp.exp(-0.5 * inner * inner) * 0.3989422804014327
        units[1, :, cells] = (inner * normal_cdf).astype(BF)
        units[0, :, cells] = (back_act * (normal_cdf + inner * density)).astype(BF)
        branch = dot(wp_t_ref[...], units[1, :, cells])
        back_norm = dot(we_t_ref[...], units[0, :, cells])
        gain_term = back_norm * whitened
        gain_ref[...] += gain_term[:, :lanes] + gain_term[:, lanes:]
        scaled = back_norm * gain
        mean_scaled = jnp.sum(scaled, axis=0, keepdims=True) * (1.0 / channels)
        mean_product = jnp.sum(scaled * whitened, axis=0, keepdims=True) * (1.0 / channels)
        back_mixed = (inv_spread * (scaled - mean_scaled - whitened * mean_product)).astype(BF)
        for k in range(2):
            r = 2 * p + k
            mask = mask_ref[pl.ds(r, 1), :].astype(F32)
            here = slice(k * lanes, (k + 1) * lanes)
            next_ref[r] = ext[r + HALO] + mask * branch[:, here]
            bm_ref[r] = back_mixed[:, here]
        return carry

    lax.fori_loop(0, rows // 2, pair_step, 0, unroll=True)
    send_edges(place_ref, [bm_ref[r].astype(F32) for r in range(rows)], bnear_ref, bfar_ref)
    core = lax.axis_index("lat") % 2
    for out, which in ((own_ref, core), (other_ref, 1 - core)):
        out[...] = nt_dot(units[which], sides[which]).astype(out.dtype)


def taps_body(
    place_ref,
    m_ref,
    near_ref,
    far_ref,
    wings_ref,
    bm_ref,
    gain_ref,
    own_ref,
    other_ref,
    ext,
    upstream,
    sums,
    moved,
):
    rows, channels, lanes = m_ref.shape
    fill_extended(ext, place_ref, m_ref, near_ref, far_ref)
    for r in range(rows):
        upstream[r] = bm_ref[r].astype(F32)
    lane = lax.broadcasted_iota(jnp.int32, (8, lanes), 1)
    ones = jnp.ones((lanes, lanes), BF)

    def step(block, carry):
        start = pl.multiple_of(block * 8, 8)
        back = upstream[:, pl.ds(start, 8), :]
        mid, wings = ext[:, pl.ds(start, 8), :], wings_ref[:, pl.ds(start, 8), :]
        result = jnp.zeros((8, lanes), F32)
        for b, (shift, value) in enumerate(joined(mid, wings)):
            turned = pltpu.roll(back, shift % lanes, 2) if shift else back
            terms = [jnp.sum(turned * value[a : a + rows], axis=0) for a in range(TAPS)]
            terms.append(gain_ref[pl.ds(start, 8), :])
            totals = dot(jnp.concatenate(terms, axis=0).astype(BF), ones)
            for a in range(TAPS):
                result = jnp.where(lane == a * TAPS + b, totals[8 * a : 8 * a + 8], result)
        result = jnp.where(lane == TAPS * TAPS, totals[8 * TAPS :], result)
        sums[pl.ds(start, 8), :] = result
        return carry

    lax.fori_loop(0, channels // 8, step, 0, unroll=True)
    block, wide = own_ref.shape
    row = lax.broadcasted_iota(jnp.int32, (2 * block, lanes), 0)
    col = lax.broadcasted_iota(jnp.int32, (2 * block, lanes), 1)
    second, inside = row // block, row % block

    def picked(first_row, first_tap, count):
        tap = inside - first_row + first_tap + second * HALF_TAPS
        pick = (col == tap) & (inside >= first_row) & (inside < first_row + count)
        return nt_dot(jnp.where(pick, 1.0, 0.0).astype(BF), moved[...].astype(BF))

    moved[...] = jnp.zeros_like(moved)
    moved[:channels, :] = sums[...]
    turned = picked(block - 1 - WHOLE_ROWS, 0, WHOLE_ROWS)
    moved[...] = jnp.zeros_like(moved)
    cut = channels // 4
    for q in range(4):
        moved[SPARE_LANE : SPARE_LANE + cut, :] = sums[q * cut : (q + 1) * cut, :]
        turned = turned + picked(q * CUT_ROWS, WHOLE_ROWS, CUT_ROWS)
    first = is_first(place_ref, (block, wide))
    own_ref[...] = jnp.where(first, turned[:block], turned[block:])
    other_ref[...] = jnp.where(first, turned[block:], turned[:block]).astype(BF)


def message_body(own_ref, got_ref, out_ref, total, piece):
    hidden, deep = own_ref.shape
    share = hidden // out_ref.shape[0]
    total[...] = own_ref[...] + got_ref[...].astype(F32)
    piece[...] = jnp.zeros_like(piece)
    for k in range(out_ref.shape[0]):
        piece[:share, :deep] = total[k * share : (k + 1) * share, :]
        out_ref[k] = piece[...].astype(BF)


def add_taps_body(rows_ref, taps_ref, taps_got_ref, out_ref):
    taps = taps_ref[...] + taps_got_ref[...].astype(F32)
    for k in range(out_ref.shape[0]):
        out_ref[k] = (rows_ref[k].astype(F32) + taps).astype(BF)


def sum_body(parts_ref, out_ref):
    total = parts_ref[0].astype(F32)
    for k in range(1, parts_ref.shape[0]):
        total = total + parts_ref[k].astype(F32)
    total = total.astype(BF)
    for k in range(out_ref.shape[0]):
        out_ref[k] = total


def final_body(parts_ref, ge_ref, gp_ref, gk_ref, gg_ref, gb_ref, halves):
    share, channels = ge_ref.shape
    _, depth, wide = parts_ref.shape
    for k in range(2):
        total = parts_ref[k].astype(F32)
        for j in range(k + 2, parts_ref.shape[0], 2):
            total = total + parts_ref[j].astype(F32)
        halves[k] = total
    ge_ref[...] = halves[0, :share, :channels]
    gp_ref[...] = halves[1, :share, :channels]
    cut = channels // 4
    lane = lax.broadcasted_iota(jnp.int32, (16, wide), 1)
    for k in range(2):
        start = k * HALF_TAPS
        whole = depth - 1 - WHOLE_ROWS
        gk_ref[start : start + WHOLE_ROWS, :] = halves[k, whole : depth - 1, :channels]
        rest = jnp.zeros((16, wide), F32)
        for q in range(4):
            value = halves[k, q * CUT_ROWS : q * CUT_ROWS + 16, :]
            value = pltpu.roll(value, (q * cut - SPARE_LANE) % wide, 1)
            rest = jnp.where((lane >= q * cut) & (lane < (q + 1) * cut), value, rest)
        count = min(CUT_ROWS, TAPS * TAPS - start - WHOLE_ROWS)
        start = start + WHOLE_ROWS
        gk_ref[start : start + count, :] = rest[:count, :channels]
    gg_ref[...] = rest[CUT_ROWS - 1 : CUT_ROWS, :channels]
    pick = lax.broadcasted_iota(jnp.int32, (8, wide), 1) == channels
    pick = jnp.where(pick, 1.0, 0.0).astype(BF)
    high = halves[0].astype(BF)
    low = (halves[0] - high.astype(F32)).astype(BF)
    gb_ref[...] = (nt_dot(pick, high) + nt_dot(pick, low))[:1, :share]


def next_body(rows_ref, out_ref, flat):
    channels, rows, lanes = out_ref.shape
    for r in range(rows):
        flat[pl.ds(r, channels, stride=rows), :] = rows_ref[r]
    out_ref[...] = flat[...].reshape(channels, rows, lanes).astype(BF)


def backward_body(
    place_ref,
    bm_ref,
    near_ref,
    far_ref,
    lon_near_ref,
    lon_far_ref,
    mask_ref,
    g_ref,
    taps_ref,
    out_ref,
    ext,
    edge,
    back,
    flat,
    spread,
):
    rows, channels, lanes = bm_ref.shape
    spread_body(taps_ref, spread)
    fill_extended(ext, place_ref, bm_ref, near_ref, far_ref)
    edge[...] = lon_edges(place_ref, lon_near_ref, lon_far_ref)

    def step(block, carry):
        start = pl.multiple_of(block * 8, 8)
        wings = line_up(edge, start, ext.shape[0])
        back[:, pl.ds(start, 8), :] = convolve(ext, wings, spread, start, rows, True)
        return carry

    lax.fori_loop(0, channels // 8, step, 0, unroll=5)
    for r in range(rows):
        mask = mask_ref[r : r + 1, :].astype(F32)
        flat[pl.ds(r, channels, stride=rows), :] = g_ref[r].astype(F32) + mask * back[r]
    out_ref[...] = flat[...].reshape(channels, rows, lanes).astype(BF)


def swap_lon(pack):
    size = lax.axis_size("lon")
    near = [(i, i ^ 1) for i in range(size)]
    far = [(i, ((i ^ 1) + (2 if i % 2 else -2)) % size) for i in range(size)]
    from_far = lax.ppermute(pack, "lon", far)
    return lax.ppermute(pack, "lon", near), from_far


def swap_lat(first, second):
    size = lax.axis_size("lat")
    near = [(i, i ^ 1) for i in range(size)]
    far = [(i, ((i ^ 1) + (2 if i % 2 else -2)) % size) for i in range(size)]
    return lax.ppermute(second, "lat", near), lax.ppermute(first, "lat", far)


def shards(
    ocean_state, land_sea, depth_kernel, norm_gain, w_expand, b_expand, w_project, cotangent
):
    channels, rows, lanes = ocean_state.shape
    hidden = w_expand.shape[0]
    n_lon, n_lat = lax.axis_size("lon"), lax.axis_size("lat")
    share = hidden // n_lon
    deep = -(-(channels + 3) // 16) * 16
    depth = share + WHOLE_ROWS + 1
    wide = 256
    cells = rows * lanes
    full = (rows, channels, lanes)
    edges = (HALO, channels, lanes)
    tile = (channels, lanes)
    flat = pltpu.VMEM((channels * rows, lanes), F32)
    ext_s = pltpu.VMEM((rows + 2 * HALO, channels, lanes), F32)
    edge_s = pltpu.VMEM(tile, F32)
    lat = lax.axis_index("lat")
    kind = lax.broadcasted_iota(jnp.int32, (8, 256), 0)
    value = jnp.where(kind == 0, 1 - lat % 2, jnp.where(kind == 1, lat, n_lat - 1 - lat))
    value = jnp.where(kind == 3, 1 - lax.axis_index("lon") % 2, value)
    place = jnp.where(kind == 4, 1 - lat // 2 % 2, value).astype(F32)
    swap = [(i, i ^ 1) for i in range(n_lat)]
    masked, near, far, pack = kernel_call(
        state_body, [(full, BF), (edges, BF), (edges, BF), (tile, BF)], [flat], n_in=3
    )(land_sea, ocean_state, place)
    lon_near, lon_far = swap_lon(pack)
    near, far = swap_lat(far, near)
    (own_edges,) = kernel_call(edges_body, [(tile, BF)], n_in=3)(place, lon_near, lon_far)
    (gated,) = kernel_call(gated_body, [(full, BF)], [flat], n_in=2)(land_sea, cotangent)
    later = (depth_kernel, norm_gain, b_expand, w_expand.T, w_project.T)
    own_edges, later = lax.optimization_barrier((own_edges, later))
    edge_near, edge_far = swap_lat(own_edges, own_edges)
    spread, gains, biases, we, wp = kernel_call(
        weights_body,
        [
            ((TAPS * TAPS, *tile), F32),
            (tile, F32),
            ((hidden, lanes), F32),
            ((hidden, channels), BF),
            ((hidden, channels), BF),
        ],
        n_in=5,
        micros=3,
    )(*later)
    we_t, wp_t = later[3:]
    next_rows, back_mixed, bnear, bfar, gain, own, other, wings = kernel_call(
        main_body,
        [
            (full, F32),
            (full, BF),
            (edges, BF),
            (edges, BF),
            (tile, F32),
            ((hidden, deep), F32),
            ((hidden, deep), BF),
            ((rows + 2 * HALO, channels, lanes), F32),
        ],
        [
            ext_s,
            edge_s,
            pltpu.VMEM(full, F32),
            pltpu.VMEM((2, hidden, cells), BF),
            pltpu.VMEM((2, deep, cells), BF),
        ],
        n_in=16,
        micros=12,
    )(
        place,
        masked,
        near,
        far,
        own_edges,
        edge_near,
        edge_far,
        land_sea,
        gated,
        spread,
        gains,
        biases,
        we,
        wp,
        we_t,
        wp_t,
    )
    got = lax.ppermute(other, "lat", swap)
    bnear, bfar = swap_lat(bfar, bnear)
    taps_own, taps_other = kernel_call(
        taps_body,
        [((depth, wide), F32), ((depth, wide), BF)],
        [ext_s, pltpu.VMEM(full, F32), edge_s, pltpu.VMEM((wide, lanes), F32)],
        n_in=7,
        micros=6,
    )(place, masked, near, far, wings, back_mixed, gain)
    got, taps_other = lax.optimization_barrier((got, taps_other))
    taps_got = lax.ppermute(taps_other, "lat", swap)
    (message,) = kernel_call(
        message_body,
        [((n_lon, depth, wide), BF)],
        [pltpu.VMEM((hidden, deep), F32), pltpu.VMEM((depth, wide), F32)],
        n_in=2,
    )(own, got)
    (message,) = kernel_call(add_taps_body, [((n_lon, depth, wide), BF)], n_in=3)(
        message, taps_own, taps_got
    )
    (back_pack,) = kernel_call(pack_body, [(tile, BF)], n_in=4)(
        place, back_mixed, bnear, bfar
    )
    back_pack, next_rows = lax.optimization_barrier((back_pack, next_rows))
    blon_near, blon_far = swap_lon(back_pack)
    (next_state,) = kernel_call(next_body, [((channels, rows, lanes), BF)], [flat], n_in=1)(
        next_rows
    )
    parts = lax.all_to_all(message, "lon", 0, 0)
    (copies,) = kernel_call(sum_body, [((n_lat, depth, wide), BF)], n_in=1)(parts)
    parts = lax.all_to_all(copies, "lat", 0, 0)
    (grad_state,) = kernel_call(
        backward_body,
        [((channels, rows, lanes), BF)],
        [ext_s, edge_s, pltpu.VMEM(full, F32), flat, pltpu.VMEM((TAPS * TAPS, *tile), F32)],
        n_in=9,
        micros=8,
    )(
        place, back_mixed, bnear, bfar, blon_near, blon_far, land_sea, gated, depth_kernel
    )
    parts, grad_state = lax.optimization_barrier((parts, grad_state))

    grad_expand, grad_project, grad_kernel, grad_gain, grad_bias = kernel_call(
        final_body,
        [
            ((share, channels), F32),
            ((share, channels), F32),
            ((TAPS * TAPS, channels), F32),
            ((1, channels), F32),
            ((1, share), F32),
        ],
        [pltpu.VMEM((2, depth, wide), F32)],
        n_in=1,
    )(parts)
    return (
        next_state,
        grad_state,
        grad_kernel,
        grad_gain.reshape(channels),
        grad_expand,
        grad_project,
        grad_bias.reshape(share),
    )


def solution(mesh):
    placed = (
        P(None, "lat", "lon"),
        P("lat", "lon"),
        P(),
        P(),
        P(),
        P(),
        P(),
        P(None, "lat", "lon"),
    )
    return jax.shard_map(
        shards,
        mesh=mesh,
        in_specs=placed,
        out_specs=(
            P(None, "lat", "lon"),
            P(None, "lat", "lon"),
            P(),
            P(),
            P("lon", None),
            P("lon", None),
            P("lon"),
        ),
        check_vma=False,
    )
```

```python
import functools

import jax
import jax.numpy as jnp
from jax import lax
from jax.experimental import pallas as pl
from jax.experimental.pallas import tpu as pltpu
from jax.sharding import PartitionSpec as P

EPS = 1e-06
BF = jnp.bfloat16
F32 = jnp.float32
HALO = 3
TAPS = 7
HALF_TAPS = 25
WHOLE_ROWS = 13
CUT_ROWS = 12
SPARE_LANE = 204
VMEM_BYTES = 16 * 1024 * 1024


def kernel_call(body, outs, scratch=(), n_in=0, n_any=0, micros=1):
    specs = [pl.BlockSpec(memory_space=pltpu.HBM)] * n_any
    specs += [pl.BlockSpec(memory_space=pltpu.VMEM)] * n_in
    return pl.pallas_call(
        body,
        out_shape=[jax.ShapeDtypeStruct(shape, dtype) for shape, dtype in outs],
        in_specs=specs,
        out_specs=[pl.BlockSpec(memory_space=pltpu.VMEM)] * len(outs),
        scratch_shapes=list(scratch),
        compiler_params=pltpu.CompilerParams(vmem_limit_bytes=VMEM_BYTES),
        cost_estimate=pl.CostEstimate(
            flops=micros * 1_000_000_000, bytes_accessed=micros * 3_000_000, transcendentals=0
        ),
    )


def nt_dot(left, right):
    return lax.dot_general(left, right, (((1,), (1,)), ((), ())), preferred_element_type=F32)


def tn_dot(left, right):
    return lax.dot_general(left, right, (((0,), (0,)), ((), ())), preferred_element_type=F32)


def dot(left, right):
    return jnp.dot(left, right, preferred_element_type=F32)


def by_rows(field_ref, flat):
    channels, rows, lanes = field_ref.shape
    flat[: channels * rows, :] = field_ref[...].astype(F32).reshape(channels * rows, lanes)
    return [flat[pl.ds(row, channels, stride=rows), :] for row in range(rows)]


def state_body(mask_ref, x_ref, place_ref, m_ref, near_ref, far_ref, pack_ref, flat):
    rows = mask_ref.shape[0]
    masked = by_rows(x_ref, flat)
    masked = [value * mask_ref[r : r + 1, :].astype(F32) for r, value in enumerate(masked)]
    pack_ref[...] = packed_edges(masked, HALO).astype(BF)
    send_edges(place_ref, masked, near_ref, far_ref)
    for row in range(rows):
        m_ref[row] = masked[row].astype(BF)


def send_edges(place_ref, values, near_ref, far_ref):
    first = is_first(place_ref, values[0].shape)
    for r in range(HALO):
        top, bottom = values[r], values[len(values) - HALO + r]
        near_ref[r] = jnp.where(first, bottom, top).astype(BF)
        far_ref[r] = jnp.where(first, top, bottom).astype(BF)


def gated_body(mask_ref, cot_ref, g_ref, flat):
    for row, value in enumerate(by_rows(cot_ref, flat)):
        g_ref[row] = (value * mask_ref[row : row + 1, :].astype(F32)).astype(BF)


def spread_body(taps_ref, spread_ref):
    count, channels, lanes = spread_ref.shape
    unit = lax.broadcasted_iota(jnp.int32, (count, lanes), 0)
    unit = unit == lax.broadcasted_iota(jnp.int32, (count, lanes), 1)
    taps = tn_dot(taps_ref[...], jnp.where(unit, 1.0, 0.0).astype(BF))
    for tap in range(count):
        spread_ref[tap] = jnp.broadcast_to(taps[:, tap : tap + 1], (channels, lanes))


def columns(row, lanes):
    high = row.astype(BF)
    rest = row - high.astype(F32)
    middle = rest.astype(BF)
    low = (rest - middle.astype(F32)).astype(BF)
    spare = jnp.zeros((5, row.shape[1]), F32)
    parts = [high.astype(F32), middle.astype(F32), low.astype(F32), spare]
    parts = jnp.concatenate(parts, axis=0).astype(BF)
    return tn_dot(parts, jnp.ones((8, lanes), BF))


def weights_body(
    taps_ref, gain_ref, bias_ref, we_in_ref, wp_in_ref, spread_ref, gains_ref, biases_ref, we_ref, wp_ref
):
    count, channels, lanes = spread_ref.shape
    spread_body(taps_ref, spread_ref)
    gains_ref[...] = columns(gain_ref[...].reshape(1, channels), lanes)
    biases_ref[...] = columns(bias_ref[...].reshape(1, bias_ref.shape[0]), lanes)
    we_ref[...] = we_in_ref[...].astype(F32).T.astype(BF)
    wp_ref[...] = wp_in_ref[...].astype(F32).T.astype(BF)


def flag(place_ref, row, shape):
    return jnp.broadcast_to(place_ref[row : row + 1, : shape[1]], shape) > 0.0


def is_first(place_ref, shape):
    return flag(place_ref, 0, shape)


def extended_rows(place_ref, mid_ref, near_ref, far_ref):
    shape = mid_ref.shape[1:]
    first = is_first(place_ref, shape)
    has_up = jnp.broadcast_to(place_ref[1:2, : shape[1]], shape) > 0.0
    has_down = jnp.broadcast_to(place_ref[2:3, : shape[1]], shape) > 0.0
    near = [near_ref[r].astype(F32) for r in range(HALO)]
    far = [far_ref[r].astype(F32) for r in range(HALO)]
    for r in range(HALO):
        yield jnp.where(has_up, jnp.where(first, far[r], near[r]), 0.0)
    for r in range(mid_ref.shape[0]):
        yield mid_ref[r].astype(F32)
    for r in range(HALO):
        yield jnp.where(has_down, jnp.where(first, near[r], far[r]), 0.0)


def packed_edges(values, first_row):
    shape = values[0].shape
    lanes = shape[1]
    lane = lax.broadcasted_iota(jnp.int32, shape, 1)
    packed = jnp.zeros(shape, F32)
    for r, value in enumerate(values, first_row):
        if r:
            value = pltpu.roll(value, 8 * r, 1)
        packed = jnp.where(((lane + (HALO - 8 * r)) & (lanes - 1)) < 2 * HALO, value, packed)
    return packed


def pack_body(place_ref, mid_ref, near_ref, far_ref, out_ref):
    rows = extended_rows(place_ref, mid_ref, near_ref, far_ref)
    out_ref[...] = packed_edges(list(rows), 0).astype(BF)


def lon_edges(place_ref, lon_near_ref, lon_far_ref):
    shape = lon_near_ref.shape
    lane = lax.broadcasted_iota(jnp.int32, shape, 1)
    side = jnp.where((lane & 7) >= 4, 1.0, 0.0)
    near_is_right = jnp.broadcast_to(place_ref[3:4, : shape[1]], shape)
    near = lon_near_ref[...].astype(F32)
    return jnp.where(side != near_is_right, near, lon_far_ref[...].astype(F32))


def edges_body(place_ref, lon_near_ref, lon_far_ref, out_ref):
    out_ref[...] = lon_edges(place_ref, lon_near_ref, lon_far_ref).astype(BF)


def all_edges(place_ref, own_ref, near_ref, far_ref):
    shape = own_ref.shape
    first = is_first(place_ref, shape)
    near, far = near_ref[...].astype(F32), far_ref[...].astype(F32)
    up = jnp.where(flag(place_ref, 1, shape), jnp.where(first, far, near), 0.0)
    down = jnp.where(flag(place_ref, 2, shape), jnp.where(first, near, far), 0.0)
    lane = lax.broadcasted_iota(jnp.int32, shape, 1)
    row = ((lane + HALO) >> 3) & 15
    others = pltpu.roll(jnp.where(row < 8, down, up), 64, 1)
    return jnp.where((row >= HALO) & (row < HALO + 8), own_ref[...].astype(F32), others)


def fill_extended(ext, place_ref, mid_ref, near_ref, far_ref):
    for r, value in enumerate(extended_rows(place_ref, mid_ref, near_ref, far_ref)):
        ext[r] = value


def line_up(edge, start, n_rows):
    ends = edge[pl.ds(start, 8), :]
    lanes = ends.shape[1]
    return jnp.stack(
        [ends] + [pltpu.roll(ends, lanes - 8 * r, 1) for r in range(1, n_rows)], axis=0
    )


def joined(mid, wings):
    lanes = mid.shape[2]
    lane = lax.broadcasted_iota(jnp.int32, mid.shape[1:], 1)
    for shift in range(-HALO, HALO + 1):
        if shift == 0:
            yield shift, mid
            continue
        outside = lane < shift if shift > 0 else lane >= lanes + shift
        yield shift, jnp.where(outside[None], wings, mid)


def convolve(ext, wings, spread_ref, start, rows, flipped):
    lanes = ext.shape[2]
    mid = ext[:, pl.ds(start, 8), :]
    total = jnp.zeros((rows, 8, lanes), F32)
    for b, (shift, value) in enumerate(joined(mid, wings)):
        window = pltpu.roll(value, -shift % lanes, 2) if shift else value
        for a in range(TAPS):
            tap = a * TAPS + b
            if flipped:
                tap = TAPS * TAPS - 1 - tap
            total = total + spread_ref[tap, pl.ds(start, 8), :][None] * window[a : a + rows]
    return total


def main_body(
    place_ref,
    m_ref,
    near_ref,
    far_ref,
    edge_own_ref,
    edge_near_ref,
    edge_far_ref,
    mask_ref,
    g_ref,
    spread_ref,
    gains_ref,
    biases_ref,
    we_ref,
    wp_ref,
    we_t_ref,
    wp_t_ref,
    next_ref,
    bm_ref,
    bnear_ref,
    bfar_ref,
    gain_ref,
    own_ref,
    other_ref,
    wings_ref,
    ext,
    edge,
    mixed,
    units,
    sides,
):
    rows, channels, lanes = m_ref.shape
    hidden, deep = own_ref.shape
    pair = 2 * lanes
    fill_extended(ext, place_ref, m_ref, near_ref, far_ref)
    edge[...] = all_edges(place_ref, edge_own_ref, edge_near_ref, edge_far_ref)

    def conv_step(block, carry):
        start = pl.multiple_of(block * 8, 8)
        wings = line_up(edge, start, ext.shape[0])
        wings_ref[:, pl.ds(start, 8), :] = wings
        mixed[:, pl.ds(start, 8), :] = convolve(ext, wings, spread_ref, start, rows, False)
        return carry

    lax.fori_loop(0, channels // 8, conv_step, 0, unroll=5)
    for r in range(rows):
        sides[1, :, r * lanes : (r + 1) * lanes] = jnp.concatenate(
            [g_ref[r].astype(F32), jnp.zeros((deep - channels, lanes), F32)], axis=0
        ).astype(BF)
    gain_ref[...] = jnp.zeros_like(gain_ref)
    tail_row = lax.broadcasted_iota(jnp.int32, (deep - channels, pair), 0)
    ones_rows = jnp.where(tail_row == 0, 1.0, 0.0)

    def pair_step(p, carry):
        cells = pl.ds(pl.multiple_of(p * pair, pair), pair)
        value = jnp.concatenate([mixed[2 * p], mixed[2 * p + 1]], axis=1)
        gain = jnp.concatenate([gains_ref[...]] * 2, axis=1)
        center = jnp.sum(value, axis=0, keepdims=True) * (1.0 / channels)
        centered = value - center
        spread = jnp.sum(centered * centered, axis=0, keepdims=True) * (1.0 / channels)
        inv_spread = lax.rsqrt(spread + EPS)
        whitened = centered * inv_spread
        normed = whitened * gain
        sides[0, :, cells] = jnp.concatenate([normed, ones_rows], axis=0).astype(BF)
        normed = normed.astype(BF)
        gated = jnp.concatenate([g_ref[2 * p], g_ref[2 * p + 1]], axis=1)
        inner = dot(we_ref[...], normed) + jnp.concatenate([biases_ref[...]] * 2, axis=1)
        back_act = dot(wp_ref[...], gated)
        normal_cdf = 0.5 * (1.0 + lax.erf(inner * 0.7071067811865476))
        density = jnp.exp(-0.5 * inner * inner) * 0.3989422804014327
        units[1, :, cells] = (inner * normal_cdf).astype(BF)
        units[0, :, cells] = (back_act * (normal_cdf + inner * density)).astype(BF)
        branch = dot(wp_t_ref[...], units[1, :, cells])
        back_norm = dot(we_t_ref[...], units[0, :, cells])
        gain_term = back_norm * whitened
        gain_ref[...] += gain_term[:, :lanes] + gain_term[:, lanes:]
        scaled = back_norm * gain
        mean_scaled = jnp.sum(scaled, axis=0, keepdims=True) * (1.0 / channels)
        mean_product = jnp.sum(scaled * whitened, axis=0, keepdims=True) * (1.0 / channels)
        back_mixed = (inv_spread * (scaled - mean_scaled - whitened * mean_product)).astype(BF)
        for k in range(2):
            r = 2 * p + k
            mask = mask_ref[pl.ds(r, 1), :].astype(F32)
            here = slice(k * lanes, (k + 1) * lanes)
            next_ref[r] = ext[r + HALO] + mask * branch[:, here]
            bm_ref[r] = back_mixed[:, here]
        return carry

    lax.fori_loop(0, rows // 2, pair_step, 0, unroll=True)
    send_edges(place_ref, [bm_ref[r].astype(F32) for r in range(rows)], bnear_ref, bfar_ref)
    core = lax.axis_index("lat") % 2
    for out, which in ((own_ref, core), (other_ref, 1 - core)):
        out[...] = nt_dot(units[which], sides[which]).astype(out.dtype)


def taps_body(
    place_ref,
    m_ref,
    near_ref,
    far_ref,
    wings_ref,
    bm_ref,
    gain_ref,
    own_ref,
    other_ref,
    ext,
    upstream,
    sums,
    moved,
):
    rows, channels, lanes = m_ref.shape
    fill_extended(ext, place_ref, m_ref, near_ref, far_ref)
    for r in range(rows):
        upstream[r] = bm_ref[r].astype(F32)
    lane = lax.broadcasted_iota(jnp.int32, (8, lanes), 1)
    ones = jnp.ones((lanes, lanes), BF)

    def step(block, carry):
        start = pl.multiple_of(block * 8, 8)
        back = upstream[:, pl.ds(start, 8), :]
        mid, wings = ext[:, pl.ds(start, 8), :], wings_ref[:, pl.ds(start, 8), :]
        result = jnp.zeros((8, lanes), F32)
        for b, (shift, value) in enumerate(joined(mid, wings)):
            turned = pltpu.roll(back, shift % lanes, 2) if shift else back
            terms = [jnp.sum(turned * value[a : a + rows], axis=0) for a in range(TAPS)]
            terms.append(gain_ref[pl.ds(start, 8), :])
            totals = dot(jnp.concatenate(terms, axis=0).astype(BF), ones)
            for a in range(TAPS):
                result = jnp.where(lane == a * TAPS + b, totals[8 * a : 8 * a + 8], result)
        result = jnp.where(lane == TAPS * TAPS, totals[8 * TAPS :], result)
        sums[pl.ds(start, 8), :] = result
        return carry

    lax.fori_loop(0, channels // 8, step, 0, unroll=True)
    block, wide = own_ref.shape
    row = lax.broadcasted_iota(jnp.int32, (2 * block, lanes), 0)
    col = lax.broadcasted_iota(jnp.int32, (2 * block, lanes), 1)
    second, inside = row // block, row % block

    def picked(first_row, first_tap, count):
        tap = inside - first_row + first_tap + second * HALF_TAPS
        pick = (col == tap) & (inside >= first_row) & (inside < first_row + count)
        return nt_dot(jnp.where(pick, 1.0, 0.0).astype(BF), moved[:wide, :].astype(BF))

    moved[...] = jnp.zeros_like(moved)
    moved[:channels, :] = sums[:channels, :]
    turned = picked(block - 1 - WHOLE_ROWS, 0, WHOLE_ROWS)
    moved[...] = jnp.zeros_like(moved)
    cut = channels // 4
    for q in range(4):
        moved[SPARE_LANE : SPARE_LANE + cut, :] = sums[q * cut : (q + 1) * cut, :]
        turned = turned + picked(q * CUT_ROWS, WHOLE_ROWS, CUT_ROWS)
    first = is_first(place_ref, (block, wide))
    own_ref[...] = jnp.where(first, turned[:block], turned[block:])
    other_ref[...] = jnp.where(first, turned[block:], turned[:block]).astype(BF)


def message_body(own_ref, got_ref, out_ref, total, piece):
    hidden, deep = own_ref.shape
    share = hidden // out_ref.shape[0]
    total[:hidden, :] = own_ref[...] + got_ref[...].astype(F32)
    piece[...] = jnp.zeros_like(piece)
    for k in range(out_ref.shape[0]):
        piece[:share, :deep] = total[k * share : (k + 1) * share, :]
        out_ref[k] = piece[...].astype(BF)


def add_taps_body(rows_ref, taps_ref, taps_got_ref, out_ref):
    taps = taps_ref[...] + taps_got_ref[...].astype(F32)
    for k in range(out_ref.shape[0]):
        out_ref[k] = (rows_ref[k].astype(F32) + taps).astype(BF)


def sum_body(parts_ref, out_ref):
    total = parts_ref[0].astype(F32)
    for k in range(1, parts_ref.shape[0]):
        total = total + parts_ref[k].astype(F32)
    total = total.astype(BF)
    for k in range(out_ref.shape[0]):
        out_ref[k] = total


def final_body(parts_ref, ge_ref, gp_ref, gk_ref, gg_ref, gb_ref, halves, taps):
    share, channels = ge_ref.shape
    _, depth, wide = parts_ref.shape
    for k in range(2):
        total = parts_ref[k].astype(F32)
        for j in range(k + 2, parts_ref.shape[0], 2):
            total = total + parts_ref[j].astype(F32)
        halves[k, :depth, :] = total
    ge_ref[...] = halves[0, :share, :channels]
    gp_ref[...] = halves[1, :share, :channels]
    cut = channels // 4
    lane = lax.broadcasted_iota(jnp.int32, (16, wide), 1)
    for k in range(2):
        start = k * HALF_TAPS
        whole = depth - 1 - WHOLE_ROWS
        taps[start : start + WHOLE_ROWS, :] = halves[k, whole : depth - 1, :]
        rest = jnp.zeros((16, wide), F32)
        for q in range(4):
            value = halves[k, q * CUT_ROWS : q * CUT_ROWS + 16, :]
            value = pltpu.roll(value, (q * cut - SPARE_LANE) % wide, 1)
            rest = jnp.where((lane >= q * cut) & (lane < (q + 1) * cut), value, rest)
        start = start + WHOLE_ROWS
        taps[start : start + 16, :] = rest
    gk_ref[...] = taps[: TAPS * TAPS, :channels]
    gg_ref[...] = rest[CUT_ROWS - 1 : CUT_ROWS, :channels]
    pick = lax.broadcasted_iota(jnp.int32, (8, wide), 1) == channels
    pick = jnp.where(pick, 1.0, 0.0).astype(BF)
    rows = halves[0, :depth, :]
    high = rows.astype(BF)
    low = (rows - high.astype(F32)).astype(BF)
    gb_ref[...] = (nt_dot(pick, high) + nt_dot(pick, low))[:1, :share]


def next_body(rows_ref, out_ref, flat):
    channels, rows, lanes = out_ref.shape
    for r in range(rows):
        flat[pl.ds(r, channels, stride=rows), :] = rows_ref[r]
    out_ref[...] = flat[: channels * rows, :].reshape(channels, rows, lanes).astype(BF)


def backward_body(
    place_ref,
    bm_ref,
    near_ref,
    far_ref,
    lon_near_ref,
    lon_far_ref,
    mask_ref,
    g_ref,
    taps_ref,
    out_ref,
    ext,
    edge,
    back,
    flat,
    spread,
):
    rows, channels, lanes = bm_ref.shape
    spread_body(taps_ref, spread)
    fill_extended(ext, place_ref, bm_ref, near_ref, far_ref)
    edge[...] = lon_edges(place_ref, lon_near_ref, lon_far_ref)

    def step(block, carry):
        start = pl.multiple_of(block * 8, 8)
        wings = line_up(edge, start, ext.shape[0])
        back[:, pl.ds(start, 8), :] = convolve(ext, wings, spread, start, rows, True)
        return carry

    lax.fori_loop(0, channels // 8, step, 0, unroll=5)
    for r in range(rows):
        mask = mask_ref[r : r + 1, :].astype(F32)
        flat[pl.ds(r, channels, stride=rows), :] = g_ref[r].astype(F32) + mask * back[r]
    out_ref[...] = flat[: channels * rows, :].reshape(channels, rows, lanes).astype(BF)


def swap_lon(pack):
    size = lax.axis_size("lon")
    near = [(i, i ^ 1) for i in range(size)]
    far = [(i, ((i ^ 1) + (2 if i % 2 else -2)) % size) for i in range(size)]
    from_far = lax.ppermute(pack, "lon", far)
    return lax.ppermute(pack, "lon", near), from_far


def swap_lat(first, second):
    size = lax.axis_size("lat")
    near = [(i, i ^ 1) for i in range(size)]
    far = [(i, ((i ^ 1) + (2 if i % 2 else -2)) % size) for i in range(size)]
    return lax.ppermute(second, "lat", near), lax.ppermute(first, "lat", far)


def shards(
    ocean_state, land_sea, depth_kernel, norm_gain, w_expand, b_expand, w_project, cotangent
):
    channels, rows, lanes = ocean_state.shape
    hidden = w_expand.shape[0]
    n_lon, n_lat = lax.axis_size("lon"), lax.axis_size("lat")
    share = hidden // n_lon
    deep = -(-(channels + 3) // 16) * 16
    depth = share + WHOLE_ROWS + 1
    wide = 256
    cells = rows * lanes
    full = (rows, channels, lanes)
    edges = (HALO, channels, lanes)
    tile = (channels, lanes)
    flat = pltpu.VMEM(((channels + 1) * rows, lanes), F32)
    ext_s = pltpu.VMEM((rows + 2 * HALO, channels, lanes), F32)
    edge_s = pltpu.VMEM(tile, F32)
    lat = lax.axis_index("lat")
    kind = lax.broadcasted_iota(jnp.int32, (8, 256), 0)
    value = jnp.where(kind == 0, 1 - lat % 2, jnp.where(kind == 1, lat, n_lat - 1 - lat))
    value = jnp.where(kind == 3, 1 - lax.axis_index("lon") % 2, value)
    place = jnp.where(kind == 4, 1 - lat // 2 % 2, value).astype(F32)
    swap = [(i, i ^ 1) for i in range(n_lat)]
    masked, near, far, pack = kernel_call(
        state_body, [(full, BF), (edges, BF), (edges, BF), (tile, BF)], [flat], n_in=3
    )(land_sea, ocean_state, place)
    lon_near, lon_far = swap_lon(pack)
    near, far = swap_lat(far, near)
    (own_edges,) = kernel_call(edges_body, [(tile, BF)], n_in=3)(place, lon_near, lon_far)
    (gated,) = kernel_call(gated_body, [(full, BF)], [flat], n_in=2)(land_sea, cotangent)
    later = (depth_kernel, norm_gain, b_expand, w_expand.T, w_project.T)
    own_edges, later = lax.optimization_barrier((own_edges, later))
    edge_near, edge_far = swap_lat(own_edges, own_edges)
    spread, gains, biases, we, wp = kernel_call(
        weights_body,
        [
            ((TAPS * TAPS, *tile), F32),
            (tile, F32),
            ((hidden, lanes), F32),
            ((hidden, channels), BF),
            ((hidden, channels), BF),
        ],
        n_in=5,
        micros=3,
    )(*later)
    we_t, wp_t = later[3:]
    next_rows, back_mixed, bnear, bfar, gain, own, other, wings = kernel_call(
        main_body,
        [
            (full, F32),
            (full, BF),
            (edges, BF),
            (edges, BF),
            (tile, F32),
            ((hidden, deep), F32),
            ((hidden, deep), BF),
            ((rows + 2 * HALO, channels, lanes), F32),
        ],
        [
            ext_s,
            edge_s,
            pltpu.VMEM(full, F32),
            pltpu.VMEM((2, hidden, cells), BF),
            pltpu.VMEM((2, deep, cells), BF),
        ],
        n_in=16,
        micros=12,
    )(
        place,
        masked,
        near,
        far,
        own_edges,
        edge_near,
        edge_far,
        land_sea,
        gated,
        spread,
        gains,
        biases,
        we,
        wp,
        we_t,
        wp_t,
    )
    got = lax.ppermute(other, "lat", swap)
    bnear, bfar = swap_lat(bfar, bnear)
    taps_own, taps_other = kernel_call(
        taps_body,
        [((depth, wide), F32), ((depth, wide), BF)],
        [
            ext_s,
            pltpu.VMEM(full, F32),
            pltpu.VMEM((channels + 16, lanes), F32),
            pltpu.VMEM((wide + 16, lanes), F32),
        ],
        n_in=7,
        micros=6,
    )(place, masked, near, far, wings, back_mixed, gain)
    got, taps_other = lax.optimization_barrier((got, taps_other))
    taps_got = lax.ppermute(taps_other, "lat", swap)
    (message,) = kernel_call(
        message_body,
        [((n_lon, depth, wide), BF)],
        [pltpu.VMEM((hidden + 16, deep), F32), pltpu.VMEM((depth, wide), F32)],
        n_in=2,
    )(own, got)
    (message,) = kernel_call(add_taps_body, [((n_lon, depth, wide), BF)], n_in=3)(
        message, taps_own, taps_got
    )
    (back_pack,) = kernel_call(pack_body, [(tile, BF)], n_in=4)(
        place, back_mixed, bnear, bfar
    )
    back_pack, next_rows = lax.optimization_barrier((back_pack, next_rows))
    blon_near, blon_far = swap_lon(back_pack)
    (next_state,) = kernel_call(next_body, [((channels, rows, lanes), BF)], [flat], n_in=1)(
        next_rows
    )
    parts = lax.all_to_all(message, "lon", 0, 0)
    (copies,) = kernel_call(sum_body, [((n_lat, depth, wide), BF)], n_in=1)(parts)
    parts = lax.all_to_all(copies, "lat", 0, 0)
    (grad_state,) = kernel_call(
        backward_body,
        [((channels, rows, lanes), BF)],
        [ext_s, edge_s, pltpu.VMEM(full, F32), flat, pltpu.VMEM((TAPS * TAPS, *tile), F32)],
        n_in=9,
        micros=8,
    )(
        place, back_mixed, bnear, bfar, blon_near, blon_far, land_sea, gated, depth_kernel
    )
    parts, grad_state = lax.optimization_barrier((parts, grad_state))

    grad_expand, grad_project, grad_kernel, grad_gain, grad_bias = kernel_call(
        final_body,
        [
            ((share, channels), F32),
            ((share, channels), F32),
            ((TAPS * TAPS, channels), F32),
            ((1, channels), F32),
            ((1, share), F32),
        ],
        [pltpu.VMEM((2, depth + 16, wide), F32), pltpu.VMEM((depth + 16, wide), F32)],
        n_in=1,
    )(parts)
    return (
        next_state,
        grad_state,
        grad_kernel,
        grad_gain.reshape(channels),
        grad_expand,
        grad_project,
        grad_bias.reshape(share),
    )


def solution(mesh):
    placed = (
        P(None, "lat", "lon"),
        P("lat", "lon"),
        P(),
        P(),
        P(),
        P(),
        P(),
        P(None, "lat", "lon"),
    )
    return jax.shard_map(
        shards,
        mesh=mesh,
        in_specs=placed,
        out_specs=(
            P(None, "lat", "lon"),
            P(None, "lat", "lon"),
            P(),
            P(),
            P("lon", None),
            P("lon", None),
            P("lon"),
        ),
        check_vma=False,
    )
```

```python
import functools

import jax
import jax.numpy as jnp
from jax import lax
from jax.experimental import pallas as pl
from jax.experimental.pallas import tpu as pltpu
from jax.sharding import PartitionSpec as P

EPS = 1e-06
BF = jnp.bfloat16
F32 = jnp.float32
HALO = 3
TAPS = 7
HALF_TAPS = 25
WHOLE_ROWS = 13
CUT_ROWS = 12
SPARE_LANE = 204
VMEM_BYTES = 16 * 1024 * 1024


def kernel_call(body, outs, scratch=(), n_in=0, n_any=0, micros=1):
    specs = [pl.BlockSpec(memory_space=pltpu.HBM)] * n_any
    specs += [pl.BlockSpec(memory_space=pltpu.VMEM)] * n_in
    return pl.pallas_call(
        body,
        out_shape=[jax.ShapeDtypeStruct(shape, dtype) for shape, dtype in outs],
        in_specs=specs,
        out_specs=[pl.BlockSpec(memory_space=pltpu.VMEM)] * len(outs),
        scratch_shapes=list(scratch),
        compiler_params=pltpu.CompilerParams(vmem_limit_bytes=VMEM_BYTES),
        cost_estimate=pl.CostEstimate(
            flops=micros * 1_000_000_000, bytes_accessed=micros * 3_000_000, transcendentals=0
        ),
    )


def nt_dot(left, right):
    return lax.dot_general(left, right, (((1,), (1,)), ((), ())), preferred_element_type=F32)


def tn_dot(left, right):
    return lax.dot_general(left, right, (((0,), (0,)), ((), ())), preferred_element_type=F32)


def dot(left, right):
    return jnp.dot(left, right, preferred_element_type=F32)


def by_rows(field_ref, flat):
    channels, rows, lanes = field_ref.shape
    flat[: channels * rows, :] = field_ref[...].astype(F32).reshape(channels * rows, lanes)
    return [flat[pl.ds(row, channels, stride=rows), :] for row in range(rows)]


def state_body(mask_ref, x_ref, place_ref, m_ref, near_ref, far_ref, pack_ref, flat):
    rows = mask_ref.shape[0]
    masked = by_rows(x_ref, flat)
    masked = [value * mask_ref[r : r + 1, :].astype(F32) for r, value in enumerate(masked)]
    pack_ref[...] = packed_edges(masked, HALO).astype(BF)
    send_edges(place_ref, masked, near_ref, far_ref)
    for row in range(rows):
        m_ref[row] = masked[row].astype(BF)


def send_edges(place_ref, values, near_ref, far_ref):
    first = is_first(place_ref, values[0].shape)
    for r in range(HALO):
        top, bottom = values[r], values[len(values) - HALO + r]
        near_ref[r] = jnp.where(first, bottom, top).astype(BF)
        far_ref[r] = jnp.where(first, top, bottom).astype(BF)


def gated_body(mask_ref, cot_ref, g_ref, flat):
    for row, value in enumerate(by_rows(cot_ref, flat)):
        g_ref[row] = (value * mask_ref[row : row + 1, :].astype(F32)).astype(BF)


def spread_body(taps_ref, spread_ref):
    count, channels, lanes = spread_ref.shape
    unit = lax.broadcasted_iota(jnp.int32, (count, lanes), 0)
    unit = unit == lax.broadcasted_iota(jnp.int32, (count, lanes), 1)
    taps = tn_dot(taps_ref[...], jnp.where(unit, 1.0, 0.0).astype(BF))
    for tap in range(count):
        spread_ref[tap] = jnp.broadcast_to(taps[:, tap : tap + 1], (channels, lanes))


def columns(row, lanes):
    high = row.astype(BF)
    rest = row - high.astype(F32)
    middle = rest.astype(BF)
    low = (rest - middle.astype(F32)).astype(BF)
    spare = jnp.zeros((5, row.shape[1]), F32)
    parts = [high.astype(F32), middle.astype(F32), low.astype(F32), spare]
    parts = jnp.concatenate(parts, axis=0).astype(BF)
    return tn_dot(parts, jnp.ones((8, lanes), BF))


def weights_body(
    taps_ref, gain_ref, bias_ref, we_in_ref, wp_in_ref, spread_ref, gains_ref, biases_ref, we_ref, wp_ref
):
    count, channels, lanes = spread_ref.shape
    spread_body(taps_ref, spread_ref)
    gains_ref[...] = columns(gain_ref[...].reshape(1, channels), lanes)
    biases_ref[...] = columns(bias_ref[...].reshape(1, bias_ref.shape[0]), lanes)
    we_ref[...] = we_in_ref[...].astype(F32).T.astype(BF)
    wp_ref[...] = wp_in_ref[...].astype(F32).T.astype(BF)


def flag(place_ref, row, shape):
    return jnp.broadcast_to(place_ref[row : row + 1, : shape[1]], shape) > 0.0


def is_first(place_ref, shape):
    return flag(place_ref, 0, shape)


def extended_rows(place_ref, mid_ref, near_ref, far_ref):
    shape = mid_ref.shape[1:]
    first = is_first(place_ref, shape)
    has_up = jnp.broadcast_to(place_ref[1:2, : shape[1]], shape) > 0.0
    has_down = jnp.broadcast_to(place_ref[2:3, : shape[1]], shape) > 0.0
    near = [near_ref[r].astype(F32) for r in range(HALO)]
    far = [far_ref[r].astype(F32) for r in range(HALO)]
    for r in range(HALO):
        yield jnp.where(has_up, jnp.where(first, far[r], near[r]), 0.0)
    for r in range(mid_ref.shape[0]):
        yield mid_ref[r].astype(F32)
    for r in range(HALO):
        yield jnp.where(has_down, jnp.where(first, near[r], far[r]), 0.0)


def packed_edges(values, first_row):
    shape = values[0].shape
    lanes = shape[1]
    lane = lax.broadcasted_iota(jnp.int32, shape, 1)
    packed = jnp.zeros(shape, F32)
    for r, value in enumerate(values, first_row):
        if r:
            value = pltpu.roll(value, 8 * r, 1)
        packed = jnp.where(((lane + (HALO - 8 * r)) & (lanes - 1)) < 2 * HALO, value, packed)
    return packed


def pack_body(place_ref, mid_ref, near_ref, far_ref, out_ref):
    rows = extended_rows(place_ref, mid_ref, near_ref, far_ref)
    out_ref[...] = packed_edges(list(rows), 0).astype(BF)


def lon_edges(place_ref, lon_near_ref, lon_far_ref):
    shape = lon_near_ref.shape
    lane = lax.broadcasted_iota(jnp.int32, shape, 1)
    side = jnp.where((lane & 7) >= 4, 1.0, 0.0)
    near_is_right = jnp.broadcast_to(place_ref[3:4, : shape[1]], shape)
    near = lon_near_ref[...].astype(F32)
    return jnp.where(side != near_is_right, near, lon_far_ref[...].astype(F32))


def edges_body(place_ref, lon_near_ref, lon_far_ref, out_ref):
    out_ref[...] = lon_edges(place_ref, lon_near_ref, lon_far_ref).astype(BF)


def all_edges(place_ref, own_ref, near_ref, far_ref):
    shape = own_ref.shape
    first = is_first(place_ref, shape)
    near, far = near_ref[...].astype(F32), far_ref[...].astype(F32)
    up = jnp.where(flag(place_ref, 1, shape), jnp.where(first, far, near), 0.0)
    down = jnp.where(flag(place_ref, 2, shape), jnp.where(first, near, far), 0.0)
    lane = lax.broadcasted_iota(jnp.int32, shape, 1)
    row = ((lane + HALO) >> 3) & 15
    others = pltpu.roll(jnp.where(row < 8, down, up), 64, 1)
    return jnp.where((row >= HALO) & (row < HALO + 8), own_ref[...].astype(F32), others)


def fill_extended(ext, place_ref, mid_ref, near_ref, far_ref):
    for r, value in enumerate(extended_rows(place_ref, mid_ref, near_ref, far_ref)):
        ext[r] = value


def line_up(edge, wings):
    channels, lanes = edge.shape
    spare = jnp.zeros((-channels % 16, lanes), F32)
    edge = jnp.concatenate([edge, spare], axis=0).astype(BF)
    for r in range(wings.shape[0]):
        turned = pltpu.roll(edge, lanes - 8 * r, 1) if r else edge
        wings[r] = turned.astype(F32)[:channels]


def joined(mid, wings):
    lanes = mid.shape[2]
    lane = lax.broadcasted_iota(jnp.int32, mid.shape[1:], 1)
    for shift in range(-HALO, HALO + 1):
        if shift == 0:
            yield shift, mid
            continue
        outside = lane < shift if shift > 0 else lane >= lanes + shift
        yield shift, jnp.where(outside[None], wings, mid)


def convolve(ext, wings, spread_ref, start, rows, flipped):
    lanes = ext.shape[2]
    mid = ext[:, pl.ds(start, 8), :]
    total = jnp.zeros((rows, 8, lanes), F32)
    for b, (shift, value) in enumerate(joined(mid, wings)):
        window = pltpu.roll(value, -shift % lanes, 2) if shift else value
        for a in range(TAPS):
            tap = a * TAPS + b
            if flipped:
                tap = TAPS * TAPS - 1 - tap
            total = total + spread_ref[tap, pl.ds(start, 8), :][None] * window[a : a + rows]
    return total


def main_body(
    place_ref,
    m_ref,
    near_ref,
    far_ref,
    edge_own_ref,
    edge_near_ref,
    edge_far_ref,
    mask_ref,
    g_ref,
    spread_ref,
    gains_ref,
    biases_ref,
    we_ref,
    wp_ref,
    we_t_ref,
    wp_t_ref,
    next_ref,
    bm_ref,
    bnear_ref,
    bfar_ref,
    gain_ref,
    own_ref,
    other_ref,
    wings_ref,
    ext,
    mixed,
    units,
    sides,
):
    rows, channels, lanes = m_ref.shape
    hidden, deep = own_ref.shape
    pair = 2 * lanes
    fill_extended(ext, place_ref, m_ref, near_ref, far_ref)
    line_up(all_edges(place_ref, edge_own_ref, edge_near_ref, edge_far_ref), wings_ref)

    def conv_step(block, carry):
        start = pl.multiple_of(block * 8, 8)
        wings = wings_ref[:, pl.ds(start, 8), :]
        mixed[:, pl.ds(start, 8), :] = convolve(ext, wings, spread_ref, start, rows, False)
        return carry

    lax.fori_loop(0, channels // 8, conv_step, 0, unroll=5)
    for r in range(rows):
        sides[1, :, r * lanes : (r + 1) * lanes] = jnp.concatenate(
            [g_ref[r].astype(F32), jnp.zeros((deep - channels, lanes), F32)], axis=0
        ).astype(BF)
    gain_ref[...] = jnp.zeros_like(gain_ref)
    tail_row = lax.broadcasted_iota(jnp.int32, (deep - channels, pair), 0)
    ones_rows = jnp.where(tail_row == 0, 1.0, 0.0)

    def pair_step(p, carry):
        cells = pl.ds(pl.multiple_of(p * pair, pair), pair)
        value = jnp.concatenate([mixed[2 * p], mixed[2 * p + 1]], axis=1)
        gain = jnp.concatenate([gains_ref[...]] * 2, axis=1)
        center = jnp.sum(value, axis=0, keepdims=True) * (1.0 / channels)
        centered = value - center
        spread = jnp.sum(centered * centered, axis=0, keepdims=True) * (1.0 / channels)
        inv_spread = lax.rsqrt(spread + EPS)
        whitened = centered * inv_spread
        normed = whitened * gain
        sides[0, :, cells] = jnp.concatenate([normed, ones_rows], axis=0).astype(BF)
        normed = normed.astype(BF)
        gated = jnp.concatenate([g_ref[2 * p], g_ref[2 * p + 1]], axis=1)
        inner = dot(we_ref[...], normed) + jnp.concatenate([biases_ref[...]] * 2, axis=1)
        back_act = dot(wp_ref[...], gated)
        normal_cdf = 0.5 * (1.0 + lax.erf(inner * 0.7071067811865476))
        density = jnp.exp(-0.5 * inner * inner) * 0.3989422804014327
        units[1, :, cells] = (inner * normal_cdf).astype(BF)
        units[0, :, cells] = (back_act * (normal_cdf + inner * density)).astype(BF)
        branch = dot(wp_t_ref[...], units[1, :, cells])
        back_norm = dot(we_t_ref[...], units[0, :, cells])
        gain_term = back_norm * whitened
        gain_ref[...] += gain_term[:, :lanes] + gain_term[:, lanes:]
        scaled = back_norm * gain
        mean_scaled = jnp.sum(scaled, axis=0, keepdims=True) * (1.0 / channels)
        mean_product = jnp.sum(scaled * whitened, axis=0, keepdims=True) * (1.0 / channels)
        back_mixed = (inv_spread * (scaled - mean_scaled - whitened * mean_product)).astype(BF)
        for k in range(2):
            r = 2 * p + k
            mask = mask_ref[pl.ds(r, 1), :].astype(F32)
            here = slice(k * lanes, (k + 1) * lanes)
            next_ref[r] = ext[r + HALO] + mask * branch[:, here]
            bm_ref[r] = back_mixed[:, here]
        return carry

    lax.fori_loop(0, rows // 2, pair_step, 0, unroll=True)
    send_edges(place_ref, [bm_ref[r].astype(F32) for r in range(rows)], bnear_ref, bfar_ref)
    core = lax.axis_index("lat") % 2
    for out, which in ((own_ref, core), (other_ref, 1 - core)):
        out[...] = nt_dot(units[which], sides[which]).astype(out.dtype)


def taps_body(
    place_ref,
    m_ref,
    near_ref,
    far_ref,
    wings_ref,
    bm_ref,
    gain_ref,
    own_ref,
    other_ref,
    ext,
    upstream,
    sums,
    moved,
):
    rows, channels, lanes = m_ref.shape
    fill_extended(ext, place_ref, m_ref, near_ref, far_ref)
    for r in range(rows):
        upstream[r] = bm_ref[r].astype(F32)
    lane = lax.broadcasted_iota(jnp.int32, (8, lanes), 1)
    ones = jnp.ones((lanes, lanes), BF)

    def step(block, carry):
        start = pl.multiple_of(block * 8, 8)
        back = upstream[:, pl.ds(start, 8), :]
        mid, wings = ext[:, pl.ds(start, 8), :], wings_ref[:, pl.ds(start, 8), :]
        result = jnp.zeros((8, lanes), F32)
        for b, (shift, value) in enumerate(joined(mid, wings)):
            turned = pltpu.roll(back, shift % lanes, 2) if shift else back
            terms = [jnp.sum(turned * value[a : a + rows], axis=0) for a in range(TAPS)]
            terms.append(gain_ref[pl.ds(start, 8), :])
            totals = dot(jnp.concatenate(terms, axis=0).astype(BF), ones)
            for a in range(TAPS):
                result = jnp.where(lane == a * TAPS + b, totals[8 * a : 8 * a + 8], result)
        result = jnp.where(lane == TAPS * TAPS, totals[8 * TAPS :], result)
        sums[pl.ds(start, 8), :] = result
        return carry

    lax.fori_loop(0, channels // 8, step, 0, unroll=True)
    block, wide = own_ref.shape
    row = lax.broadcasted_iota(jnp.int32, (2 * block, lanes), 0)
    col = lax.broadcasted_iota(jnp.int32, (2 * block, lanes), 1)
    second, inside = row // block, row % block

    def picked(first_row, first_tap, count):
        tap = inside - first_row + first_tap + second * HALF_TAPS
        pick = (col == tap) & (inside >= first_row) & (inside < first_row + count)
        return nt_dot(jnp.where(pick, 1.0, 0.0).astype(BF), moved[:wide, :].astype(BF))

    moved[...] = jnp.zeros_like(moved)
    moved[:channels, :] = sums[:channels, :]
    turned = picked(block - 1 - WHOLE_ROWS, 0, WHOLE_ROWS)
    moved[...] = jnp.zeros_like(moved)
    cut = channels // 4
    for q in range(4):
        moved[SPARE_LANE : SPARE_LANE + cut, :] = sums[q * cut : (q + 1) * cut, :]
        turned = turned + picked(q * CUT_ROWS, WHOLE_ROWS, CUT_ROWS)
    first = is_first(place_ref, (block, wide))
    own_ref[...] = jnp.where(first, turned[:block], turned[block:])
    other_ref[...] = jnp.where(first, turned[block:], turned[:block]).astype(BF)


def message_body(own_ref, got_ref, out_ref, total, piece):
    hidden, deep = own_ref.shape
    share = hidden // out_ref.shape[0]
    total[:hidden, :] = own_ref[...] + got_ref[...].astype(F32)
    piece[...] = jnp.zeros_like(piece)
    for k in range(out_ref.shape[0]):
        piece[:share, :deep] = total[k * share : (k + 1) * share, :]
        out_ref[k] = piece[...].astype(BF)


def add_taps_body(rows_ref, taps_ref, taps_got_ref, out_ref):
    taps = taps_ref[...] + taps_got_ref[...].astype(F32)
    for k in range(out_ref.shape[0]):
        out_ref[k] = (rows_ref[k].astype(F32) + taps).astype(BF)


def sum_body(parts_ref, out_ref):
    total = parts_ref[0].astype(F32)
    for k in range(1, parts_ref.shape[0]):
        total = total + parts_ref[k].astype(F32)
    total = total.astype(BF)
    for k in range(out_ref.shape[0]):
        out_ref[k] = total


def final_body(parts_ref, ge_ref, gp_ref, gk_ref, gg_ref, gb_ref, halves, taps):
    share, channels = ge_ref.shape
    _, depth, wide = parts_ref.shape
    for k in range(2):
        total = parts_ref[k].astype(F32)
        for j in range(k + 2, parts_ref.shape[0], 2):
            total = total + parts_ref[j].astype(F32)
        halves[k, :depth, :] = total
    ge_ref[...] = halves[0, :share, :channels]
    gp_ref[...] = halves[1, :share, :channels]
    cut = channels // 4
    lane = lax.broadcasted_iota(jnp.int32, (16, wide), 1)
    for k in range(2):
        start = k * HALF_TAPS
        whole = depth - 1 - WHOLE_ROWS
        taps[start : start + WHOLE_ROWS, :] = halves[k, whole : depth - 1, :]
        rest = jnp.zeros((16, wide), F32)
        for q in range(4):
            value = halves[k, q * CUT_ROWS : q * CUT_ROWS + 16, :]
            value = pltpu.roll(value, (q * cut - SPARE_LANE) % wide, 1)
            rest = jnp.where((lane >= q * cut) & (lane < (q + 1) * cut), value, rest)
        start = start + WHOLE_ROWS
        taps[start : start + 16, :] = rest
    gk_ref[...] = taps[: TAPS * TAPS, :channels]
    gg_ref[...] = rest[CUT_ROWS - 1 : CUT_ROWS, :channels]
    pick = lax.broadcasted_iota(jnp.int32, (8, wide), 1) == channels
    pick = jnp.where(pick, 1.0, 0.0).astype(BF)
    rows = halves[0, :depth, :]
    high = rows.astype(BF)
    low = (rows - high.astype(F32)).astype(BF)
    gb_ref[...] = (nt_dot(pick, high) + nt_dot(pick, low))[:1, :share]


def next_body(rows_ref, out_ref, flat):
    channels, rows, lanes = out_ref.shape
    for r in range(rows):
        flat[pl.ds(r, channels, stride=rows), :] = rows_ref[r]
    out_ref[...] = flat[: channels * rows, :].reshape(channels, rows, lanes).astype(BF)


def backward_body(
    place_ref,
    bm_ref,
    near_ref,
    far_ref,
    lon_near_ref,
    lon_far_ref,
    mask_ref,
    g_ref,
    taps_ref,
    out_ref,
    ext,
    wings,
    back,
    flat,
    spread,
):
    rows, channels, lanes = bm_ref.shape
    spread_body(taps_ref, spread)
    fill_extended(ext, place_ref, bm_ref, near_ref, far_ref)
    line_up(lon_edges(place_ref, lon_near_ref, lon_far_ref), wings)

    def step(block, carry):
        start = pl.multiple_of(block * 8, 8)
        here = wings[:, pl.ds(start, 8), :]
        back[:, pl.ds(start, 8), :] = convolve(ext, here, spread, start, rows, True)
        return carry

    lax.fori_loop(0, channels // 8, step, 0, unroll=5)
    for r in range(rows):
        mask = mask_ref[r : r + 1, :].astype(F32)
        flat[pl.ds(r, channels, stride=rows), :] = g_ref[r].astype(F32) + mask * back[r]
    out_ref[...] = flat[: channels * rows, :].reshape(channels, rows, lanes).astype(BF)


def swap_lon(pack):
    size = lax.axis_size("lon")
    near = [(i, i ^ 1) for i in range(size)]
    far = [(i, ((i ^ 1) + (2 if i % 2 else -2)) % size) for i in range(size)]
    from_far = lax.ppermute(pack, "lon", far)
    return lax.ppermute(pack, "lon", near), from_far


def swap_lat(first, second):
    size = lax.axis_size("lat")
    near = [(i, i ^ 1) for i in range(size)]
    far = [(i, ((i ^ 1) + (2 if i % 2 else -2)) % size) for i in range(size)]
    return lax.ppermute(second, "lat", near), lax.ppermute(first, "lat", far)


def shards(
    ocean_state, land_sea, depth_kernel, norm_gain, w_expand, b_expand, w_project, cotangent
):
    channels, rows, lanes = ocean_state.shape
    hidden = w_expand.shape[0]
    n_lon, n_lat = lax.axis_size("lon"), lax.axis_size("lat")
    share = hidden // n_lon
    deep = -(-(channels + 3) // 16) * 16
    depth = share + WHOLE_ROWS + 1
    wide = 256
    cells = rows * lanes
    full = (rows, channels, lanes)
    edges = (HALO, channels, lanes)
    tile = (channels, lanes)
    flat = pltpu.VMEM(((channels + 1) * rows, lanes), F32)
    ext_s = pltpu.VMEM((rows + 2 * HALO, channels, lanes), F32)
    lat = lax.axis_index("lat")
    kind = lax.broadcasted_iota(jnp.int32, (8, 256), 0)
    value = jnp.where(kind == 0, 1 - lat % 2, jnp.where(kind == 1, lat, n_lat - 1 - lat))
    value = jnp.where(kind == 3, 1 - lax.axis_index("lon") % 2, value)
    place = jnp.where(kind == 4, 1 - lat // 2 % 2, value).astype(F32)
    swap = [(i, i ^ 1) for i in range(n_lat)]
    masked, near, far, pack = kernel_call(
        state_body, [(full, BF), (edges, BF), (edges, BF), (tile, BF)], [flat], n_in=3
    )(land_sea, ocean_state, place)
    lon_near, lon_far = swap_lon(pack)
    near, far = swap_lat(far, near)
    (own_edges,) = kernel_call(edges_body, [(tile, BF)], n_in=3)(place, lon_near, lon_far)
    (gated,) = kernel_call(gated_body, [(full, BF)], [flat], n_in=2)(land_sea, cotangent)
    later = (depth_kernel, norm_gain, b_expand, w_expand.T, w_project.T)
    own_edges, later = lax.optimization_barrier((own_edges, later))
    edge_near, edge_far = swap_lat(own_edges, own_edges)
    spread, gains, biases, we, wp = kernel_call(
        weights_body,
        [
            ((TAPS * TAPS, *tile), F32),
            (tile, F32),
            ((hidden, lanes), F32),
            ((hidden, channels), BF),
            ((hidden, channels), BF),
        ],
        n_in=5,
        micros=3,
    )(*later)
    we_t, wp_t = later[3:]
    next_rows, back_mixed, bnear, bfar, gain, own, other, wings = kernel_call(
        main_body,
        [
            (full, F32),
            (full, BF),
            (edges, BF),
            (edges, BF),
            (tile, F32),
            ((hidden, deep), F32),
            ((hidden, deep), BF),
            ((rows + 2 * HALO, channels, lanes), F32),
        ],
        [
            ext_s,
            pltpu.VMEM(full, F32),
            pltpu.VMEM((2, hidden, cells), BF),
            pltpu.VMEM((2, deep, cells), BF),
        ],
        n_in=16,
        micros=12,
    )(
        place,
        masked,
        near,
        far,
        own_edges,
        edge_near,
        edge_far,
        land_sea,
        gated,
        spread,
        gains,
        biases,
        we,
        wp,
        we_t,
        wp_t,
    )
    got = lax.ppermute(other, "lat", swap)
    bnear, bfar = swap_lat(bfar, bnear)
    taps_own, taps_other = kernel_call(
        taps_body,
        [((depth, wide), F32), ((depth, wide), BF)],
        [
            ext_s,
            pltpu.VMEM(full, F32),
            pltpu.VMEM((channels + 16, lanes), F32),
            pltpu.VMEM((wide + 16, lanes), F32),
        ],
        n_in=7,
        micros=6,
    )(place, masked, near, far, wings, back_mixed, gain)
    got, taps_other = lax.optimization_barrier((got, taps_other))
    taps_got = lax.ppermute(taps_other, "lat", swap)
    (message,) = kernel_call(
        message_body,
        [((n_lon, depth, wide), BF)],
        [pltpu.VMEM((hidden + 16, deep), F32), pltpu.VMEM((depth, wide), F32)],
        n_in=2,
    )(own, got)
    (message,) = kernel_call(add_taps_body, [((n_lon, depth, wide), BF)], n_in=3)(
        message, taps_own, taps_got
    )
    (back_pack,) = kernel_call(pack_body, [(tile, BF)], n_in=4)(
        place, back_mixed, bnear, bfar
    )
    back_pack, next_rows = lax.optimization_barrier((back_pack, next_rows))
    blon_near, blon_far = swap_lon(back_pack)
    (next_state,) = kernel_call(next_body, [((channels, rows, lanes), BF)], [flat], n_in=1)(
        next_rows
    )
    parts = lax.all_to_all(message, "lon", 0, 0)
    (copies,) = kernel_call(sum_body, [((n_lat, depth, wide), BF)], n_in=1)(parts)
    parts = lax.all_to_all(copies, "lat", 0, 0)
    (grad_state,) = kernel_call(
        backward_body,
        [((channels, rows, lanes), BF)],
        [ext_s, ext_s, pltpu.VMEM(full, F32), flat, pltpu.VMEM((TAPS * TAPS, *tile), F32)],
        n_in=9,
        micros=8,
    )(
        place, back_mixed, bnear, bfar, blon_near, blon_far, land_sea, gated, depth_kernel
    )
    parts, grad_state = lax.optimization_barrier((parts, grad_state))

    grad_expand, grad_project, grad_kernel, grad_gain, grad_bias = kernel_call(
        final_body,
        [
            ((share, channels), F32),
            ((share, channels), F32),
            ((TAPS * TAPS, channels), F32),
            ((1, channels), F32),
            ((1, share), F32),
        ],
        [pltpu.VMEM((2, depth + 16, wide), F32), pltpu.VMEM((depth + 16, wide), F32)],
        n_in=1,
    )(parts)
    return (
        next_state,
        grad_state,
        grad_kernel,
        grad_gain.reshape(channels),
        grad_expand,
        grad_project,
        grad_bias.reshape(share),
    )


def solution(mesh):
    placed = (
        P(None, "lat", "lon"),
        P("lat", "lon"),
        P(),
        P(),
        P(),
        P(),
        P(),
        P(None, "lat", "lon"),
    )
    return jax.shard_map(
        shards,
        mesh=mesh,
        in_specs=placed,
        out_specs=(
            P(None, "lat", "lon"),
            P(None, "lat", "lon"),
            P(),
            P(),
            P("lon", None),
            P("lon", None),
            P("lon"),
        ),
        check_vma=False,
    )
```
